256 devices in a mesh: row: 32 (over x, z), col: 8 (over y, core).
Axes of the slice: x: 4, y: 4, z: 8, core: 2. Of those that a mesh axis runs over, the one named last changes fastest.
Arguments:
- features: bfloat16 [65536, 128], P(('col', 'row')), may hold values from -6 to 6
- node_ids: int32 [256, 256], P(('col', 'row')), may hold values from 0 to 255, each once within a row
- edge_blocks: bfloat16 [64, 128, 128], replicated, may hold values from -0.25 to 0.25
- block_rows: int32 [32, 8, 256], P('row', 'col'), may hold values from 0 to 15
- block_cols: int32 [32, 8, 256], P('row', 'col'), may hold values from 0 to 63
- block_ids: int32 [32, 8, 256], P('row', 'col'), may hold values from 0 to 63
- live_blocks: int32 [32, 8], P('row', 'col'), may hold values from 1 to 256, as said below
- weight: bfloat16 [128, 256], replicated, may hold values from -0.5 to 0.5
- bias: float32 [256], replicated, may hold values from -4 to 4
- cotangent: bfloat16 [65536, 256], P(('row', 'col')), may hold values from -6 to 6
Outputs:
- layer_out: float32 [65536, 256], P(('row', 'col'))
- feature_grad: float32 [65536, 128], P(('col', 'row'))
- weight_grad: float32 [128, 256], replicated
- bias_grad: float32 [256], replicated
The draws below stay inside these ranges and needn't reach their ends.
Inputs may be any that keep to these rules, and one draw needn't show every extreme that they name: Only the first live_blocks[r, c] slots of grid cell (r, c) hold blocks; some grid cell uses all 256 slots in every draw.
All inputs are finite; a program needn't handle non-finite values.
Results may differ from the reference program's by a relative error of at most 0.0003.
Values may be sent and summed in bfloat16 or wider, within the bound.
A program may use at most 128 MiB of HBM per device.

```python
import math
import jax
import jax.numpy as jnp
from jax import lax

FIN = 128
HID = 256
BLK = 128
VT = 64
BD = 2
NNZ_DEV = 256
TILE = 256
NODES = 65536
N_ROW = 32
N_COL = 8
DEVICES = 256


def draw_live_blocks(key, part):
    key = jax.random.fold_in(key, 7)
    first_key, second_key = jax.random.split(key)
    levels = jax.random.randint(first_key, (N_ROW, N_COL), 0, 64)
    counts = 1 + (NNZ_DEV - 1) * levels * levels // 3969
    chosen = jax.random.randint(second_key, (), 0, N_ROW * N_COL)
    is_chosen = jnp.arange(N_ROW * N_COL).reshape(N_ROW, N_COL) == chosen
    return jnp.where(is_chosen, NNZ_DEV, counts).astype(jnp.int32)


def plant(entries, own_key, smallest, high):
    dims = entries.shape
    place = [jax.random.randint(jax.random.fold_in(own_key, axis), (), 0, dims[axis]) for axis in range(len(dims))]
    entries = entries.at[tuple(place)].set(smallest)
    longest = dims.index(max(dims))
    place[longest] = (place[longest] + 1) % dims[longest]
    return entries.at[tuple(place)].set(high)


def block_scale(stream_key, extent, pieces, smallest, top_value):
    loudness = 1.0
    for dim, blocks in pieces:
        draws = jax.random.uniform(jax.random.fold_in(jax.random.fold_in(stream_key, 6), dim), (blocks,), jnp.float32, smallest / len(pieces), top_value / len(pieces))
        loudness = loudness * jnp.repeat(jnp.exp(draws), extent[dim] // blocks).reshape((-1,) + (1,) * (len(extent) - 1 - dim))
    return loudness


def gaussian(stream_key, extent, scale, reach, pieces=(), held_as=jnp.bfloat16):
    factor_of = block_scale(stream_key, extent, pieces, -0.22, 0.18) if pieces else 1.0
    array = jax.random.normal(stream_key, extent, jnp.float32) * scale * factor_of
    return jnp.minimum(jnp.maximum(array, -reach), reach).astype(held_as)


def setup_inputs(seed: int = 0) -> dict:
    splits = jax.random.split(jax.random.key(seed), 11)
    return {
        "features": gaussian(splits[0], (NODES, FIN), 1.0, 6.0, ((0, 256),)),
        "node_ids": jax.vmap(lambda own: jax.random.permutation(own, TILE))(jax.random.split(splits[1], DEVICES)).reshape((DEVICES, TILE)).astype(jnp.int32),
        "edge_blocks": gaussian(splits[2], (VT, BLK, BLK), (4 * BLK) ** -0.5, 0.25),
        "block_rows": plant(jax.random.randint(splits[3], (N_ROW, N_COL, NNZ_DEV), 0, BD * N_COL), jax.random.fold_in(splits[3], 1), 0, (BD * N_COL) - 1).astype(jnp.int32),
        "block_cols": plant(jax.random.randint(splits[4], (N_ROW, N_COL, NNZ_DEV), 0, BD * N_ROW), jax.random.fold_in(splits[4], 1), 0, (BD * N_ROW) - 1).astype(jnp.int32),
        "block_ids": plant(jax.random.randint(splits[5], (N_ROW, N_COL, NNZ_DEV), 0, VT), jax.random.fold_in(splits[5], 1), 0, VT - 1).astype(jnp.int32),
        "live_blocks": draw_live_blocks(jax.random.fold_in(splits[10], 71), 0),
        "weight": gaussian(splits[7], (FIN, HID), FIN ** -0.5, 0.5),
        "bias": gaussian(splits[8], (HID,), 1.0, 4.0, (), jnp.float32),
        "cotangent": gaussian(splits[9], (NODES, HID), 1.0, 6.0, ((0, 256),)),
    }


def aggregate_blocks(source, block_rows, block_cols, block_ids, live_blocks, table, transpose):
    highest = lax.Precision.HIGHEST
    columns_count = source.shape[1]
    row_span = BD * N_COL * BLK
    col_span = BD * N_ROW * BLK
    slot_index = jnp.arange(NNZ_DEV, dtype=jnp.int32)

    def visit(device_index, totals):
        grid_row = (device_index // N_COL).astype(jnp.int32)
        grid_col = (device_index % N_COL).astype(jnp.int32)
        rows_here = block_rows[grid_row, grid_col]
        cols_here = block_cols[grid_row, grid_col]
        weight_tiles = table[block_ids[grid_row, grid_col]]
        keep = (slot_index < live_blocks[grid_row, grid_col]).astype(jnp.float32)
        if transpose:
            in_start = (grid_row * row_span).astype(jnp.int32)
            out_start = (grid_col * col_span).astype(jnp.int32)
            strip_rows = lax.dynamic_slice_in_dim(source, in_start, row_span, 0).reshape(-1, BLK, columns_count)
            picked = strip_rows[rows_here]
            product = jnp.einsum('gji,gjw->giw', weight_tiles, picked, precision=highest)
            destination = cols_here
            out_span = col_span
        else:
            in_start = (grid_col * col_span).astype(jnp.int32)
            out_start = (grid_row * row_span).astype(jnp.int32)
            strip_rows = lax.dynamic_slice_in_dim(source, in_start, col_span, 0).reshape(-1, BLK, columns_count)
            picked = strip_rows[cols_here]
            product = jnp.einsum('gij,gjw->giw', weight_tiles, picked, precision=highest)
            destination = rows_here
            out_span = row_span
        product = product * keep[:, None, None]
        placed = jnp.zeros((out_span // BLK, BLK, columns_count), jnp.float32).at[destination].add(product)
        current = lax.dynamic_slice_in_dim(totals, out_start, out_span, 0)
        return lax.dynamic_update_slice_in_dim(totals, current + placed.reshape(out_span, columns_count), out_start, 0)
    start_totals = jnp.zeros((source.shape[0], columns_count), jnp.float32)
    return lax.fori_loop(0, N_ROW * N_COL, visit, start_totals)

def reference(features, node_ids, edge_blocks, block_rows, block_cols, block_ids, live_blocks, weight, bias, cotangent):
    highest = lax.Precision.HIGHEST
    table = edge_blocks.astype(jnp.float32)
    shards = features.reshape(-1, TILE, FIN)
    ordered = jnp.take_along_axis(shards, node_ids[:, :, None], axis=1).reshape(-1, FIN)
    aggregate = aggregate_blocks(ordered.astype(jnp.float32), block_rows, block_cols, block_ids, live_blocks, table, False)
    weight_wide = weight.astype(jnp.float32)
    layer_out = jnp.dot(aggregate, weight_wide, precision=highest) + bias.astype(jnp.float32)
    projected = jnp.dot(cotangent, weight.T, preferred_element_type=jnp.float32)
    grad_ordered = aggregate_blocks(projected, block_rows, block_cols, block_ids, live_blocks, table, True)
    shard_index = jnp.arange(node_ids.shape[0], dtype=jnp.int32)[:, None]
    feature_grad = jnp.zeros((node_ids.shape[0], TILE, FIN), jnp.float32)
    feature_grad = feature_grad.at[shard_index, node_ids].set(grad_ordered.reshape(-1, TILE, FIN)).reshape(-1, FIN)
    scale_factor = 1.0 / math.sqrt(NODES)
    cotangent_wide = cotangent.astype(jnp.float32)
    weight_grad = jnp.dot(aggregate.T, cotangent_wide, precision=highest) * scale_factor
    bias_grad = lax.optimization_barrier(jnp.sum(cotangent_wide, axis=0)) * scale_factor
    return (layer_out, feature_grad, weight_grad, bias_grad)
```

```python
import functools
import math

import jax
import jax.numpy as jnp
from jax import lax
from jax.experimental import pallas as pl
from jax.experimental.pallas import tpu as pltpu
from jax.sharding import PartitionSpec as P

F32 = jnp.float32
BF16 = jnp.bfloat16
MESH = pl.DeviceIdType.MESH

NX, NZ, NY, NCORE = 4, 8, 4, 2
NROW, NCOL = NX * NZ, NY * NCORE
BLK = 128
SLOTS = 256
FPAIRS = (SLOTS + 2 * NCOL) // 2
BPAIRS = (SLOTS + 2 * NROW) // 2
QLEN = 384


def iota(shape, dim):
    return lax.broadcasted_iota(jnp.int32, shape, dim).astype(F32)


def to_column(row, size):
    eye = iota((size, size), 0) == iota((size, size), 1)
    return jnp.sum(jnp.where(eye, row, 0.0), axis=1, keepdims=True)


def sort_direction(key, code, live, zero_source, empty_pair, keep_out):
    lane = iota((1, SLOTS), 1)
    key = jnp.where(lane < live, key, 1000.0)
    key_col = to_column(key, SLOTS)
    code_col = to_column(code, SLOTS)
    earlier = iota((SLOTS, SLOTS), 1) < iota((SLOTS, SLOTS), 0)
    same = jnp.where((key_col == key) & earlier, 1.0, 0.0)
    rank = jnp.sum(same, axis=1, keepdims=True)
    names = iota((SLOTS, 128), 1)
    count = jnp.sum(jnp.where(key_col == names, 1.0, 0.0), axis=0, keepdims=True)
    padded = 2.0 * jnp.floor((count + 1.0) * 0.5)
    before = jnp.sum(jnp.where(names < key_col, padded, 0.0), axis=1, keepdims=True)
    place = jnp.where(key_col < 999.0, before + rank, -1.0)
    spot = iota((SLOTS, QLEN), 1)
    picked = jnp.sum(jnp.where(place == spot, code_col, 0.0), axis=0, keepdims=True)
    picked = picked.astype(jnp.int32)
    empty = picked == 0
    ids = jnp.where(empty, 0, lax.shift_right_logical(picked - 1, 7))
    src = jnp.where(empty, zero_source, (picked - 1) & 127)
    padded_col = to_column(padded, 128)
    count_col = to_column(count, 128)
    upper = iota((128, 128), 0) < iota((128, 128), 1)
    offset = jnp.sum(jnp.where(upper, padded_col, 0.0), axis=0, keepdims=True)
    ends = jnp.where(count > 0.0, (offset + padded) * 0.5 - 1.0, float(empty_pair))
    offset_col = to_column(offset, 128)
    start_col = jnp.where(count_col > 0.0, offset_col * 0.5, -1.0)
    starts = jnp.sum(jnp.where(start_col == iota((128, QLEN), 1), 1.0, 0.0), axis=0, keepdims=True)
    keep = 1.0 - starts
    return ids, src, keep.astype(jnp.int32), ends.astype(jnp.int32)


def prep_kernel(rows_ref, cols_ref, ids_ref, live_ref, out_ref):
    live = live_ref[0, 0].astype(F32)
    rows = rows_ref[...].reshape(1, SLOTS)
    cols = cols_ref[...].reshape(1, SLOTS)
    ids = ids_ref[...].reshape(1, SLOTS)
    half = cols & 1
    dev = lax.shift_right_logical(cols, 1)
    dev_x = lax.shift_right_logical(dev, 3)
    dev_z = dev & 7
    at_a = dev_z * NX + dev_x
    where_x = jnp.where(half == 0, at_a, dev + NROW)
    f = sort_direction(
        rows.astype(F32), (ids * 128 + where_x + 1).astype(F32), live, 2 * NROW, FPAIRS, None
    )
    b = sort_direction(
        cols.astype(F32), (ids * 128 + rows + 1).astype(F32), live, 2 * NCOL, BPAIRS, None
    )
    out_ref[...] = jnp.zeros((8, QLEN), jnp.int32)
    for k in range(3):
        out_ref[k : k + 1, :] = f[k]
        out_ref[3 + k : 4 + k, :] = b[k]
    out_ref[6:7, 0:128] = f[3]
    out_ref[7:8, 0:128] = b[3]


class Counter:
    def __init__(self):
        self.n = 0

    def take(self, *dims):
        base = self.n
        self.n += math.prod(dims)

        def at(*index):
            k = 0
            for d, i in zip(dims, index):
                assert 0 <= i < d
                k = k * d + i
            return base + k

        return at


def semaphores():
    c = Counter()
    names = dict(
        ax=(4,), ar=(5, 4), al=(4, 4), br=(5,), bl=(4,), bx=(8, 4),
        cy=(4,), cs=(4,),
        ra=(4, 4), la=(3, 4), xa=(4,), rb=(4,), lb=(3,), xb=(8, 4),
        ys=(4,), yy=(4,), w1=(8,), w2=(4,), w3=(8,), w4=(4,), w5=(8,),
    )
    return {k: c.take(*d) for k, d in names.items()}, c.n


SEM, NSEM = semaphores()


def split(value):
    high = value.astype(BF16)
    low = (value - high.astype(F32)).astype(BF16)
    return high, low


def dot(a, b):
    return jnp.dot(a, b, preferred_element_type=F32)


def main_kernel(
    idx, feat, nid, edge, weight, bias, cot,
    out_ref, fg_ref, wg_ref, bg_ref,
    xs, cs, et, phl, sb, sf, ts, yb, ra_r, ra_l, xa_r, rb_r, rb_l, xb_r, ys_r, yy_r,
    wp, w1_r, w2_s, w2_r, w3_r, w4_r, w5_r, ss, rs,
):
    r = lax.axis_index("row")
    c = lax.axis_index("col")
    x, z = r // NZ, lax.rem(r, NZ)
    y, core = c // NCORE, lax.rem(c, NCORE)

    def xm(d):
        return lax.rem(x + d + NX, NX)

    def zm(d):
        return lax.rem(z + d + NZ, NZ)

    def ym(d):
        return lax.rem(y + d + NY, NY)

    def plane(px, pz):
        return (px * NZ + pz, c)

    def column(py, pc):
        return (r, py * NCORE + pc)

    def col_id(d):
        return (r, lax.rem(c + d, NCOL))

    started = []
    pending = {}

    def send(key, src, dst, dev):
        k = SEM[key[0]](*key[1:])
        d = pltpu.make_async_remote_copy(
            src_ref=src, dst_ref=dst, send_sem=ss.at[k], recv_sem=rs.at[k],
            device_id=dev, device_id_type=MESH,
        )
        d.start()
        pending[key] = d
        started.append(d)

    def recv(*key):
        pending.pop(key).wait_recv()

    barrier = pltpu.get_barrier_semaphore()
    peers = [plane(xm(d), z) for d in range(1, NX)]
    peers += [plane(x, zm(d)) for d in range(1, NZ)]
    peers += [col_id(d) for d in range(1, NCOL)]
    for p in peers:
        pl.semaphore_signal(barrier, inc=1, device_id=p, device_id_type=MESH)

    order = jnp.where(
        lax.broadcasted_iota(jnp.int32, (2 * BLK, 2 * BLK), 0) == nid[...], 1.0, 0.0
    )
    order_t = order.T.astype(BF16)
    ordered = dot(order_t, feat[...]).astype(BF16)
    xs[pl.ds(z * NX + x, 1)] = ordered[None, :BLK]
    xs[pl.ds(NROW + r, 1)] = ordered[None, BLK:]
    pl.semaphore_wait(barrier, len(peers))

    def a_at(pz, px):
        return xs.at[pz * NX + px]

    def b_at(px, pz):
        return xs.at[NROW + px * NZ + pz]

    def ag_ar(s, f):
        o = a_at(zm(1 - s), xm(-f))
        send(("ar", s, f), o, o, plane(x, zm(1)))

    def ag_al(s, f):
        o = a_at(zm(s - 1), xm(-f))
        send(("al", s, f), o, o, plane(x, zm(-1)))

    def ag_br(s):
        o = b_at(x, zm(1 - s))
        send(("br", s), o, o, plane(x, zm(1)))

    def ag_bl(s):
        o = b_at(x, zm(s - 1))
        send(("bl", s), o, o, plane(x, zm(-1)))

    def ag_bx(rel):
        o = b_at(x, zm(-rel))
        for d in range(1, NX):
            send(("bx", rel, d), o, o, plane(xm(d), z))

    mine = cs.at[c]
    for d in range(1, NY):
        send(("cy", d), cot, mine, column(ym(d), core))
    send(("cs", 0), cot, mine, column(y, 1 - core))
    ag_ar(1, 0)
    ag_al(1, 0)
    for d in range(1, NX):
        o = a_at(z, x)
        send(("ax", d), o, o, plane(xm(d), z))
    ag_br(1)
    ag_bl(1)
    ag_bx(0)
    cs[pl.ds(c, 1)] = cot[...][None]

    xs[2 * NROW] = jnp.zeros((BLK, BLK), BF16)
    phl[2 * NCOL] = jnp.zeros((BLK, 2 * BLK), BF16)
    sb[BPAIRS] = jnp.zeros((BLK, BLK), F32)
    sf[FPAIRS] = jnp.zeros((BLK, BLK), F32)

    def turn(k, carry):
        for u in range(4):
            et[4 * k + u] = edge[4 * k + u].T
        return carry

    lax.fori_loop(0, 16, turn, 0)

    for f in range(1, NX):
        recv("ax", f)
        ag_ar(1, f)
        ag_al(1, f)
    for d in range(1, NY):
        recv("cy", d)
        o = cs.at[ym(-d) * NCORE + core]
        send(("cs", d), o, o, column(y, 1 - core))

    def project(k):
        p = lax.dot_general(
            cs[k], weight[...], (((1,), (1,)), ((), ())), preferred_element_type=F32
        )
        high, low = split(p)
        both = jnp.concatenate([high, low], axis=1)
        phl[pl.ds(2 * k, 1)] = both[None, :BLK]
        phl[pl.ds(2 * k + 1, 1)] = both[None, BLK:]

    for d in range(NY):
        project(ym(-d) * NCORE + core)
    for d in range(NY):
        recv("cs", d)
    for d in range(NY):
        project(ym(-d) * NCORE + 1 - core)

    def ag_step(s):
        for f in range(NX):
            recv("ar", s, f)
            if s < 4:
                ag_ar(s + 1, f)
            if s < 4:
                recv("al", s, f)
                if s < 3:
                    ag_al(s + 1, f)
        recv("br", s)
        if s < 4:
            ag_br(s + 1)
        ag_bx(s)
        if s < 4:
            recv("bl", s)
            if s < 3:
                ag_bl(s + 1)
            ag_bx(NZ - s)

    def pair(p, base, table, source, sums, total):
        e0, e1 = idx[base, 2 * p], idx[base, 2 * p + 1]
        s0, s1 = idx[base + 1, 2 * p], idx[base + 1, 2 * p + 1]
        keep = idx[base + 2, p].astype(F32)
        left = jnp.concatenate([table[e0], table[e1]], axis=1)
        right = jnp.concatenate([source[s0], source[s1]], axis=0)
        prod = dot(left, right)
        if prod.shape[1] == 2 * BLK:
            prod = prod[:, :BLK] + prod[:, BLK:]
        total = total * keep + prod
        sums[pl.ds(p, 1)] = total[None]
        return total

    def run_pairs(lo, hi, unroll, total, base, table, source, sums):
        assert (hi - lo) % unroll == 0

        def step(k, total):
            for u in range(unroll):
                total = pair(lo + k * unroll + u, base, table, source, sums, total)
            return total

        return lax.fori_loop(0, (hi - lo) // unroll, step, total)

    zero = jnp.zeros((BLK, BLK), F32)
    ag_step(1)
    total = run_pairs(0, 40, 4, zero, 3, et, phl, sb)
    ag_step(2)
    total = run_pairs(40, 80, 4, total, 3, et, phl, sb)
    ag_step(3)
    total = run_pairs(80, 120, 4, total, 3, et, phl, sb)
    ag_step(4)
    run_pairs(120, 160, 4, total, 3, et, phl, sb)

    def stage(k, carry):
        px, pz = k // NZ, lax.rem(k, NZ)
        ts[pl.ds(pz * NX + px, 1)] = sb[idx[7, 2 * k]][None]
        ts[pl.ds(NROW + k, 1)] = sb[idx[7, 2 * k + 1]][None]
        return carry

    lax.fori_loop(0, NROW, stage, 0)

    def t_a(pz, px):
        return pz * NX + px

    def t_b(px, pz):
        return NROW + px * NZ + pz

    def add(at, *refs):
        v = ts[pl.ds(at, 1)]
        for ref in refs:
            v = v + ref[...][None]
        ts[pl.ds(at, 1)] = v

    def rs_ra(s, f):
        at = t_a(zm(4 - s), xm(f))
        if s:
            recv("ra", s - 1, f)
            add(at, ra_r.at[s - 1, f])
        send(("ra", s, f), ts.at[at], ra_r.at[s, f], plane(x, zm(1)))

    def rs_la(s, f):
        at = t_a(zm(s - 3), xm(f))
        if s:
            recv("la", s - 1, f)
            add(at, ra_l.at[s - 1, f])
        send(("la", s, f), ts.at[at], ra_l.at[s, f], plane(x, zm(-1)))

    def rs_bx(rel):
        for d in range(1, NX):
            at = t_b(xm(d), zm(rel))
            send(("xb", rel, d), ts.at[at], xb_r.at[rel, d - 1], plane(xm(d), z))

    def rs_bg(rel):
        for d in range(1, NX):
            recv("xb", rel, d)
        add(t_b(x, zm(rel)), *[xb_r.at[rel, d - 1] for d in range(1, NX)])

    def rs_rb(s):
        rs_bg((4 - s) % NZ)
        at = t_b(x, zm(4 - s))
        if s:
            recv("rb", s - 1)
            add(at, rb_r.at[s - 1])
        send(("rb", s), ts.at[at], rb_r.at[s], plane(x, zm(1)))

    def rs_lb(s):
        rs_bg((s - 3) % NZ)
        at = t_b(x, zm(s - 3))
        if s:
            recv("lb", s - 1)
            add(at, rb_l.at[s - 1])
        send(("lb", s), ts.at[at], rb_l.at[s], plane(x, zm(-1)))

    for f in range(NX):
        rs_ra(0, f)
        rs_la(0, f)
    for rel in (4, 5, 3, 6, 2, 7, 1, 0):
        rs_bx(rel)

    for rel in range(NZ):
        for d in range(1, NX):
            recv("bx", rel, d)

    total = run_pairs(0, 44, 4, zero, 0, edge, xs, sf)
    for f in range(NX):
        rs_ra(1, f)
        rs_la(1, f)
    rs_rb(0)
    rs_lb(0)
    total = run_pairs(44, 92, 4, total, 0, edge, xs, sf)
    for f in range(NX):
        rs_ra(2, f)
        rs_la(2, f)
    rs_rb(1)
    rs_lb(1)
    run_pairs(92, 136, 4, total, 0, edge, xs, sf)

    def stage_y(k, carry):
        yb[pl.ds(k, 1)] = sf[idx[6, k]][None]
        return carry

    lax.fori_loop(0, 2 * NCOL, stage_y, 0)
    for py in range(NY):
        at = 2 * (py * NCORE + 1 - core)
        send(("ys", py), yb.at[pl.ds(at, 2)], ys_r.at[py], column(y, 1 - core))

    for f in range(NX):
        rs_ra(3, f)
    rs_rb(2)
    rs_lb(2)

    def grad(k, carry):
        acc, low_sum = carry
        strip = cs[k]
        agg = yb[pl.ds(2 * k, 2)].reshape(2 * BLK, BLK)
        high, low = split(agg.T)
        acc = acc + dot(high, strip) + dot(low, strip)
        low_sum = low_sum + dot(jnp.ones((8, 2 * BLK), BF16), strip)
        return acc, low_sum

    acc, low_sum = lax.fori_loop(
        0, NCOL, grad, (jnp.zeros((BLK, 2 * BLK), F32), jnp.zeros((8, 2 * BLK), F32))
    )
    wp[...] = (acc * (1.0 / 256.0)).reshape(NCOL, 16, 2 * BLK)
    for d in range(1, NCOL):
        to = lax.rem(c + d, NCOL)
        send(("w1", d), wp.at[to], w1_r.at[d - 1], col_id(d))

    for f in range(NX):
        recv("ra", 3, f)
        recv("la", 2, f)
        add(t_a(z, xm(f)), ra_r.at[3, f], ra_l.at[2, f])
        if f:
            send(("xa", f), ts.at[t_a(z, xm(f))], xa_r.at[f - 1], plane(xm(f), z))
    rs_rb(3)

    for py in range(NY):
        recv("ys", py)
    for py in range(NY):
        at = 2 * (py * NCORE + core)
        yb[pl.ds(at, 2)] = yb[pl.ds(at, 2)] + ys_r[py]
    for d in range(1, NY):
        at = 2 * (ym(d) * NCORE + core)
        send(("yy", d), yb.at[pl.ds(at, 2)], yy_r.at[d - 1], column(ym(d), core))

    for d in range(1, NCOL):
        recv("w1", d)
    part = wp[c]
    for d in range(1, NCOL):
        part = part + w1_r[d - 1]
    low_row = low_sum[0:1] * (1.0 / 256.0)
    bias_tile = jnp.concatenate(
        [low_row[:, :BLK], low_row[:, BLK:], jnp.zeros((6, BLK), F32)], axis=0
    )
    for t in range(NX):
        a, b = 8 * (t // 2), BLK * (t % 2)
        w2_s[t, 0:8] = part[a : a + 8, b : b + BLK]
        w2_s[t, 8:16] = bias_tile
    w2_r[pl.ds(x, 1)] = w2_s[pl.ds(x, 1)]
    for d in range(1, NX):
        send(("w2", d), w2_s.at[xm(d)], w2_r.at[x], plane(xm(d), z))

    recv("rb", 3)
    recv("lb", 2)
    rs_bg(0)
    add(t_b(x, z), rb_r.at[3], rb_l.at[2])
    for f in range(1, NX):
        recv("xa", f)
    add(t_a(z, x), *[xa_r.at[f - 1] for f in range(1, NX)])

    for d in range(1, NX):
        recv("w2", d)
    w3_r[pl.ds(z, 1)] = (((w2_r[0] + w2_r[1]) + w2_r[2]) + w2_r[3])[None]
    for d in range(1, NZ):
        send(("w3", d), w3_r.at[z], w3_r.at[z], plane(x, zm(d)))

    order_b = order.astype(BF16)
    whole = jnp.concatenate([ts[t_a(z, x)], ts[t_b(x, z)]], axis=0)
    high, low = split(whole)
    fg_ref[...] = dot(order_b, high) + dot(order_b, low)

    for d in range(1, NZ):
        recv("w3", d)
    tile = w3_r[0]
    for k in range(1, NZ):
        tile = tile + w3_r[k]
    w4_r[pl.ds(x, 1)] = tile[None, 0:8]
    for d in range(1, NX):
        send(("w4", d), w4_r.at[x], w4_r.at[x], plane(xm(d), z))
    bg_ref[...] = jnp.concatenate([tile[8:9], tile[9:10]], axis=1)

    for d in range(1, NY):
        recv("yy", d)
    agg = yb[pl.ds(2 * c, 2)]
    for d in range(1, NY):
        agg = agg + yy_r[d - 1]
    high, low = split(agg.reshape(2 * BLK, BLK))
    out_ref[...] = dot(high, weight[...]) + dot(low, weight[...]) + bias[...]

    for d in range(1, NX):
        recv("w4", d)
    w5_r[pl.ds(c, 1)] = w4_r[...][None]
    for d in range(1, NCOL):
        send(("w5", d), w5_r.at[c], w5_r.at[c], col_id(d))
    for d in range(1, NCOL):
        recv("w5", d)
    for k in range(NCOL):
        for t in range(NX):
            a, b = 16 * k + 8 * (t // 2), BLK * (t % 2)
            wg_ref[a : a + 8, b : b + BLK] = w5_r[k, t]

    assert not pending, pending.keys()
    for d in started:
        d.wait_send()


def body(
    features, node_ids, edge_blocks, block_rows, block_cols, block_ids, live_blocks,
    weight, bias, cotangent,
):
    vmem = pl.BlockSpec(memory_space=pltpu.VMEM)
    smem = pl.BlockSpec(memory_space=pltpu.SMEM)
    plan = pl.pallas_call(
        prep_kernel,
        out_shape=jax.ShapeDtypeStruct((8, QLEN), jnp.int32),
        in_specs=[vmem, vmem, vmem, smem],
        out_specs=vmem,
    )(block_rows, block_cols, block_ids, live_blocks)
    tile = (BLK, BLK)
    scratch = [
        pltpu.VMEM((2 * NROW + 1, *tile), BF16),
        pltpu.VMEM((NCOL, 2 * BLK, 2 * BLK), BF16),
        pltpu.VMEM((64, *tile), BF16),
        pltpu.VMEM((2 * NCOL + 1, BLK, 2 * BLK), BF16),
        pltpu.VMEM((BPAIRS + 1, *tile), F32),
        pltpu.VMEM((FPAIRS + 1, *tile), F32),
        pltpu.VMEM((2 * NROW, *tile), F32),
        pltpu.VMEM((2 * NCOL, *tile), F32),
        pltpu.VMEM((4, 4, *tile), F32),
        pltpu.VMEM((3, 4, *tile), F32),
        pltpu.VMEM((3, *tile), F32),
        pltpu.VMEM((4, *tile), F32),
        pltpu.VMEM((3, *tile), F32),
        pltpu.VMEM((8, 3, *tile), F32),
        pltpu.VMEM((4, 2, *tile), F32),
        pltpu.VMEM((3, 2, *tile), F32),
        pltpu.VMEM((NCOL, 16, 2 * BLK), F32),
        pltpu.VMEM((NCOL - 1, 16, 2 * BLK), F32),
        pltpu.VMEM((NX, 16, BLK), F32),
        pltpu.VMEM((NX, 16, BLK), F32),
        pltpu.VMEM((NZ, 16, BLK), F32),
        pltpu.VMEM((NX, 8, BLK), F32),
        pltpu.VMEM((NCOL, NX, 8, BLK), F32),
        pltpu.SemaphoreType.DMA((NSEM,)),
        pltpu.SemaphoreType.DMA((NSEM,)),
    ]
    layer_out, feature_grad, weight_grad, bias_grad = pl.pallas_call(
        main_kernel,
        out_shape=(
            jax.ShapeDtypeStruct((2 * BLK, 2 * BLK), F32),
            jax.ShapeDtypeStruct((2 * BLK, BLK), F32),
            jax.ShapeDtypeStruct((BLK, 2 * BLK), F32),
            jax.ShapeDtypeStruct((1, 2 * BLK), F32),
        ),
        in_specs=[smem] + [vmem] * 6,
        out_specs=(vmem,) * 4,
        scratch_shapes=scratch,
        compiler_params=pltpu.CompilerParams(
            collective_id=0, has_side_effects=True, vmem_limit_bytes=58 * 2**20
        ),
    )(plan, features, node_ids, edge_blocks, weight, bias.reshape(1, -1), cotangent)
    return layer_out, feature_grad, weight_grad, bias_grad.reshape(-1)


def solution(mesh):
    return jax.shard_map(
        body,
        mesh=mesh,
        in_specs=(
            P(("col", "row"), None),
            P(("col", "row"), None),
            P(),
            P("row", "col", None),
            P("row", "col", None),
            P("row", "col", None),
            P("row", "col"),
            P(),
            P(),
            P(("row", "col"), None),
        ),
        out_specs=(P(("row", "col"), None), P(("col", "row"), None), P(), P()),
        check_vma=False,
    )
```

```python
import math

import jax
import jax.numpy as jnp
from jax import lax
from jax.experimental import pallas as pl
from jax.experimental.pallas import tpu as pltpu
from jax.sharding import PartitionSpec as P

F32 = jnp.float32
BF16 = jnp.bfloat16
I16 = jnp.int16
I32 = jnp.int32
MESH = pl.DeviceIdType.MESH

NX, NZ, NY, NCORE = 4, 8, 4, 2
NROW, NCOL = NX * NZ, NY * NCORE
NXY = NX * NY
BLK = 128
SLOTS = 256
FPAIRS = (SLOTS + 2 * NCOL) // 2
BPAIRS = (SLOTS + 2 * NROW) // 2
QLEN = 384
MSG = BLK + 16
SCALE = 1.0 / 256.0


def iota(shape, dim):
    return lax.broadcasted_iota(I32, shape, dim)


def to_column(row, size):
    eye = iota((size, size), 0) == iota((size, size), 1)
    return jnp.sum(jnp.where(eye, row, 0), axis=1, keepdims=True, dtype=I32)


def sort_direction(key, code, live, zero_source, empty_pair):
    key = jnp.where(iota((1, SLOTS), 1) < live, key, 1000)
    key_col = to_column(key, SLOTS)
    code_col = to_column(code, SLOTS)
    earlier = iota((SLOTS, SLOTS), 1) < iota((SLOTS, SLOTS), 0)
    same = jnp.where((key_col == key) & earlier, 1, 0)
    rank = jnp.sum(same, axis=1, keepdims=True, dtype=I32)
    names = iota((SLOTS, 128), 1)
    count = jnp.sum(jnp.where(key_col == names, 1, 0), axis=0, keepdims=True, dtype=I32)
    padded = (count + 1) & -2
    before = jnp.sum(jnp.where(names < key_col, padded, 0), axis=1, keepdims=True, dtype=I32)
    place = jnp.where(key_col < 999, before + rank, -1)
    spot = iota((SLOTS, QLEN), 1)
    picked = jnp.sum(jnp.where(place == spot, code_col, 0), axis=0, keepdims=True, dtype=I32)
    empty = picked == 0
    ids = jnp.where(empty, 0, lax.shift_right_logical(picked - 1, 7))
    src = jnp.where(empty, zero_source, (picked - 1) & 127)
    padded_col = to_column(padded, 128)
    count_col = to_column(count, 128)
    upper = iota((128, 128), 0) < iota((128, 128), 1)
    offset = jnp.sum(jnp.where(upper, padded_col, 0), axis=0, keepdims=True, dtype=I32)
    ends = jnp.where(count > 0, lax.shift_right_logical(offset + padded, 1) - 1, empty_pair)
    offset_col = to_column(offset, 128)
    start_col = jnp.where(count_col > 0, lax.shift_right_logical(offset_col, 1), -1)
    starts = jnp.where(start_col == iota((128, QLEN), 1), 1, 0)
    keep = 1 - jnp.sum(starts, axis=0, keepdims=True, dtype=I32)
    return ids, src, keep, ends


def plan_slots(rows_ref, cols_ref, ids_ref, live_ref, out_ref):
    live = live_ref[0, 0]
    rows = rows_ref[...].reshape(1, SLOTS)
    cols = cols_ref[...].reshape(1, SLOTS)
    ids = ids_ref[...].reshape(1, SLOTS)
    dev = lax.shift_right_logical(cols, 1)
    dev_x = lax.shift_right_logical(dev, 3)
    dev_z = dev & 7
    at_a = dev_z * NX + dev_x
    place = jnp.where((cols & 1) == 0, at_a, dev + NROW)
    f = sort_direction(rows, ids * 128 + place + 1, live, 2 * NROW, FPAIRS)
    b = sort_direction(place, ids * 128 + rows + 1, live, 2 * NCOL, BPAIRS)
    out_ref[...] = jnp.zeros((8, QLEN), I32)
    for k in range(3):
        out_ref[k : k + 1, :] = f[k]
        out_ref[3 + k : 4 + k, :] = b[k]
    out_ref[6:7, 0:128] = f[3]
    out_ref[7:8, 0:128] = b[3]


class Counter:
    def __init__(self):
        self.n = 0

    def take(self, *dims):
        base = self.n
        self.n += math.prod(dims)

        def at(*index):
            k = 0
            for d, i in zip(dims, index):
                assert 0 <= i < d
                k = k * d + i
            return base + k

        return at


def message_numbers():
    c = Counter()
    coded = dict(ra=(4, 4), la=(3, 4), xa=(3,), rb=(4,), lb=(3,), xb=(8, 3))
    plain = dict(
        ax=(4,), ar=(5, 4), al=(4, 4), br=(5,), bl=(4,), bx=(8, 4), cy=(4,), cs=(4,),
        ys=(4,), yy=(4,), g1=(1,), g2=(16,), g3=(8,), g4=(16,), g5=(1,),
    )
    table = {k: c.take(*d) for k, d in coded.items()}
    n_coded = c.n
    table.update({k: c.take(*d) for k, d in plain.items()})
    return table, n_coded, c.n


SEM, NCODED, NSEM = message_numbers()


def split(value):
    high = value.astype(BF16)
    low = (value - high.astype(F32)).astype(BF16)
    return high, low


def dot(a, b):
    return jnp.dot(a, b, preferred_element_type=F32)


def encode(value, ref):
    top = jnp.maximum(jnp.max(jnp.abs(value), axis=0, keepdims=True), 1e-30)
    e = jnp.ceil(jnp.log(top) * 256.0)
    q = jnp.round(value * (jnp.exp(e * (-1.0 / 256.0)) * 32000.0)).astype(I32)
    ref[0:BLK] = q.astype(I16)
    ref[BLK:MSG] = jnp.broadcast_to(e, (16, BLK)).astype(I32).astype(I16)


def decode(ref):
    e = ref[BLK:MSG].astype(I32).astype(F32)[0:1]
    return ref[0:BLK].astype(I32).astype(F32) * (jnp.exp(e * (1.0 / 256.0)) * (1.0 / 32000.0))


def main_kernel(
    live, rows, cols, ids, feat, nid, edge_hbm, weight, cot,
    agg_ref, gord_ref, grads_ref,
    plan_v, idx, edge, xs, cs, et, wt, sb, sf, ts, yb, sbuf, rbuf, ys_r, yy_r,
    wp, ws_r, p1_s, p1_r, p2_r, p3_r, ss, rs, ls,
):
    r = lax.axis_index("row")
    c = lax.axis_index("col")
    x, z = r // NZ, lax.rem(r, NZ)
    y, core = c // NCORE, lax.rem(c, NCORE)

    def xm(d):
        return lax.rem(x + d + NX, NX)

    def zm(d):
        return lax.rem(z + d + NZ, NZ)

    def ym(d):
        return lax.rem(y + d + NY, NY)

    def plane(px, pz):
        return (px * NZ + pz, c)

    def column(py, pc):
        return (r, py * NCORE + pc)

    def xy_peer(dx, dy):
        return (xm(dx) * NZ + z, ym(dy) * NCORE + core)

    started = []
    pending = {}

    def send(key, src, dst, dev):
        k = SEM[key[0]](*key[1:])
        d = pltpu.make_async_remote_copy(
            src_ref=src, dst_ref=dst, send_sem=ss.at[k], recv_sem=rs.at[k],
            device_id=dev, device_id_type=MESH,
        )
        d.start()
        pending[key] = d
        started.append(d)

    def recv(*key):
        pending.pop(key).wait_recv()

    xy_steps = [(a, b) for a in range(NX) for b in range(NY) if a or b]

    barrier = pltpu.get_barrier_semaphore()
    peers = [column(y, 1 - core)]
    peers += [plane(x, zm(d)) for d in (1, 7, 2, 6, 3, 5, 4)]
    peers += [xy_peer(*s) for s in xy_steps]
    for p in peers:
        pl.semaphore_signal(barrier, inc=1, device_id=p, device_id_type=MESH)
    edge_copy = pltpu.make_async_copy(edge_hbm, edge, ls.at[0])
    edge_copy.start()

    order = jnp.where(
        lax.broadcasted_iota(jnp.int32, (2 * BLK, 2 * BLK), 0) == nid[...], 1.0, 0.0
    )
    ordered = dot(order.T.astype(BF16), feat[...]).astype(BF16)
    xs[pl.ds(z * NX + x, 1)] = ordered[None, :BLK]
    xs[pl.ds(NROW + r, 1)] = ordered[None, BLK:]
    plan_slots(rows, cols, ids, live, plan_v)
    plan_copy = pltpu.make_async_copy(plan_v, idx, ls.at[1])
    plan_copy.start()
    wt[...] = weight[...].T
    pl.semaphore_wait(barrier, len(peers))

    def a_at(pz, px):
        return xs.at[pz * NX + px]

    def b_at(px, pz):
        return xs.at[NROW + px * NZ + pz]

    def ag_ar(s, f):
        o = a_at(zm(1 - s), xm(-f))
        send(("ar", s, f), o, o, plane(x, zm(1)))

    def ag_al(s, f):
        o = a_at(zm(s - 1), xm(-f))
        send(("al", s, f), o, o, plane(x, zm(-1)))

    def ag_br(s):
        o = b_at(x, zm(1 - s))
        send(("br", s), o, o, plane(x, zm(1)))

    def ag_bl(s):
        o = b_at(x, zm(s - 1))
        send(("bl", s), o, o, plane(x, zm(-1)))

    def ag_bx(rel):
        o = b_at(x, zm(-rel))
        for d in (2, 1, 3):
            send(("bx", rel, d), o, o, plane(xm(d), z))

    mine = cs.at[pl.ds(2 * c, 2)]
    for d in (2, 1, 3):
        send(("cy", d), cot, mine, column(ym(d), core))
    for d in (2, 1, 3):
        o = a_at(z, x)
        send(("ax", d), o, o, plane(xm(d), z))
    ag_ar(1, 0)
    ag_al(1, 0)
    ag_br(1)
    ag_bl(1)
    send(("cs", 0), cot, mine, column(y, 1 - core))
    ag_bx(0)
    cs[pl.ds(2 * c, 2)] = cot[...]

    xs[2 * NROW] = jnp.zeros((BLK, BLK), BF16)
    cs[2 * NCOL] = jnp.zeros((BLK, 2 * BLK), BF16)
    sb[BPAIRS] = jnp.zeros((BLK, 2 * BLK), F32)
    sf[FPAIRS] = jnp.zeros((BLK, BLK), F32)
    own_bias = jnp.sum(cot[...].reshape(2 * BLK, 2 * BLK).astype(F32), axis=0, keepdims=True) * SCALE
    bias_tile = jnp.concatenate(
        [own_bias[:, :BLK], own_bias[:, BLK:], jnp.zeros((6, BLK), F32)], axis=0
    )

    edge_copy.wait()
    plan_copy.wait()

    def turn(k, carry):
        for u in range(8):
            et[8 * k + u] = edge[8 * k + u].T
        return carry

    lax.fori_loop(0, 8, turn, 0)

    for f in (1, 3, 2):
        recv("ax", f)
        ag_ar(1, f)
        ag_al(1, f)
    for d in (1, 3, 2):
        recv("cy", d)
        o = cs.at[pl.ds(2 * (ym(-d) * NCORE + core), 2)]
        send(("cs", d), o, o, column(y, 1 - core))

    def ag_step(s):
        recv("br", s)
        if s < 4:
            ag_br(s + 1)
            recv("bl", s)
            if s < 3:
                ag_bl(s + 1)
        for f in (0, 1, 3, 2):
            recv("ar", s, f)
            if s < 4:
                ag_ar(s + 1, f)
                recv("al", s, f)
                if s < 3:
                    ag_al(s + 1, f)
        ag_bx(s)
        if s < 4:
            ag_bx(NZ - s)

    def run_pairs(lo, hi, unroll, total, body):
        assert (hi - lo) % unroll == 0

        def step(k, total):
            for u in range(unroll):
                total = body(lo + k * unroll + u, total)
            return total

        return lax.fori_loop(0, (hi - lo) // unroll, step, total)

    def back(p, total):
        e0, e1 = idx[3, 2 * p], idx[3, 2 * p + 1]
        left = jnp.concatenate([et[e0], et[e1]], axis=1)
        right = jnp.concatenate([cs[idx[4, 2 * p]], cs[idx[4, 2 * p + 1]]], axis=0)
        total = total * idx[5, p].astype(F32) + dot(left, right)
        sb[pl.ds(p, 1)] = total[None]
        return total

    def forth(p, total):
        e0, e1 = idx[0, 2 * p], idx[0, 2 * p + 1]
        left = jnp.concatenate([edge[e0], edge[e1]], axis=1)
        right = jnp.concatenate([xs[idx[1, 2 * p]], xs[idx[1, 2 * p + 1]]], axis=0)
        total = total * idx[2, p].astype(F32) + dot(left, right)
        sf[pl.ds(p, 1)] = total[None]
        return total

    ag_step(1)
    for d in range(NY):
        recv("cs", d)
    total = run_pairs(0, 80, 16, jnp.zeros((BLK, 2 * BLK), F32), back)
    ag_step(2)
    run_pairs(80, 160, 16, total, back)
    ag_step(3)

    def stage(k, carry):
        for u in range(8):
            at = 8 * k + u
            high, low = split(sb[idx[7, at]])
            ts[pl.ds(at, 1)] = (dot(high, wt[...]) + dot(low, wt[...]))[None]
        return carry

    lax.fori_loop(0, 2 * NROW // 8, stage, 0)

    def t_a(pz, px):
        return pz * NX + px

    def t_b(px, pz):
        return NROW + px * NZ + pz

    def post(key, value, dev):
        k = SEM[key[0]](*key[1:])
        encode(value, sbuf.at[k])
        send(key, sbuf.at[k], rbuf.at[k], dev)

    def take(*key):
        recv(*key)
        return decode(rbuf.at[SEM[key[0]](*key[1:])])

    def rs_ra(s, f):
        v = ts[t_a(zm(4 - s), xm(f))]
        if s:
            v = v + take("ra", s - 1, f)
        post(("ra", s, f), v, plane(x, zm(1)))

    def rs_la(s, f):
        v = ts[t_a(zm(s - 3), xm(f))]
        if s:
            v = v + take("la", s - 1, f)
        post(("la", s, f), v, plane(x, zm(-1)))

    def rs_bx(rel):
        for d in (2, 1, 3):
            post(("xb", rel, d - 1), ts[t_b(xm(d), zm(rel))], plane(xm(d), z))

    def rs_bg(rel):
        v = ts[t_b(x, zm(rel))]
        for d in range(1, NX):
            v = v + take("xb", rel, d - 1)
        return v

    def rs_rb(s):
        v = rs_bg((4 - s) % NZ)
        if s:
            v = v + take("rb", s - 1)
        post(("rb", s), v, plane(x, zm(1)))

    def rs_lb(s):
        v = rs_bg((s - 3) % NZ)
        if s:
            v = v + take("lb", s - 1)
        post(("lb", s), v, plane(x, zm(-1)))

    def rs_a(s):
        for f in range(NX):
            rs_ra(s, f)
            if s < 3:
                rs_la(s, f)

    rs_a(0)
    rs_bx(4)
    rs_bx(5)
    ag_step(4)
    for rel in (3, 6, 2, 7, 1, 0):
        rs_bx(rel)

    def grad(k, acc):
        for u in range(8):
            at = 8 * k + u
            xt = xs[at].T
            high, low = split(sb[idx[7, at]])
            acc = acc + dot(
                jnp.concatenate([xt, xt], axis=1), jnp.concatenate([high, low], axis=0)
            )
        return acc

    acc = lax.fori_loop(0, NROW // 8, grad, jnp.zeros((BLK, 2 * BLK), F32))
    for rel in range(NZ):
        for d in range(1, NX):
            recv("bx", rel, d)
    acc = lax.fori_loop(NROW // 8, 2 * NROW // 8, grad, acc) * SCALE
    for t in range(2 * NXY):
        a, b = 8 * (t // 2), BLK * (t % 2)
        wp[t // NXY, t % NXY] = acc[a : a + 8, b : b + BLK]
    send(("g1", 0), wp.at[1 - core], ws_r, column(y, 1 - core))

    rs_a(1)
    rs_rb(0)
    rs_lb(0)

    recv("g1", 0)
    me = x * NY + y
    p1_s[:, 0:8] = wp[core] + ws_r[...]
    for t in range(NXY):
        p1_s[t, 8:16] = bias_tile
    p1_r[pl.ds(me, 1)] = p1_s[pl.ds(me, 1)]
    for i, (a, b) in enumerate(xy_steps):
        send(("g2", i), p1_s.at[xm(a) * NY + ym(b)], p1_r.at[me], xy_peer(a, b))

    total = run_pairs(0, 68, 17, jnp.zeros((BLK, BLK), F32), forth)
    rs_a(2)
    rs_rb(1)
    rs_lb(1)
    for i in range(len(xy_steps)):
        recv("g2", i)
    tile = p1_r[0]
    for k in range(1, NXY):
        tile = tile + p1_r[k]
    p2_r[pl.ds(z, 1)] = tile[None]
    for d in (4, 3, 5, 2, 6, 1, 7):
        send(("g3", d), p2_r.at[z], p2_r.at[z], plane(x, zm(d)))

    run_pairs(68, 136, 17, total, forth)

    def stage_y(k, carry):
        for u in range(4):
            yb[4 * k + u] = sf[idx[6, 4 * k + u]]
        return carry

    lax.fori_loop(0, 2 * NCOL // 4, stage_y, 0)
    for py in range(NY):
        at = 2 * (py * NCORE + 1 - core)
        send(("ys", py), yb.at[pl.ds(at, 2)], ys_r.at[py], column(y, 1 - core))

    for d in range(1, NZ):
        recv("g3", d)
    tile = p2_r[0]
    for k in range(1, NZ):
        tile = tile + p2_r[k]
    p3_r[pl.ds(core, 1), pl.ds(me, 1)] = tile[None, None, 0:8]
    p3_r[pl.ds(core, 1), NXY : NXY + 1] = tile[None, None, 8:16]
    for i, (a, b) in enumerate(xy_steps):
        o = p3_r.at[core, me]
        send(("g4", i), o, o, xy_peer(a, b))

    for py in range(NY):
        recv("ys", py)
    for py in range(NY):
        at = 2 * (py * NCORE + core)
        yb[pl.ds(at, 2)] = yb[pl.ds(at, 2)] + ys_r[py]
    for d in (2, 1, 3):
        at = 2 * (ym(d) * NCORE + core)
        send(("yy", d), yb.at[pl.ds(at, 2)], yy_r.at[d - 1], column(ym(d), core))

    rs_a(3)
    rs_rb(2)
    rs_lb(2)

    own_a = None
    for f in (1, 2, 3, 0):
        v = ts[t_a(z, xm(f))] + take("ra", 3, f) + take("la", 2, f)
        if f:
            post(("xa", f - 1), v, plane(xm(f), z))
        else:
            own_a = v
    rs_rb(3)
    own_b = rs_bg(0) + take("lb", 2)

    for i in range(len(xy_steps)):
        recv("g4", i)
    o = p3_r.at[core]
    send(("g5", 0), o, o, column(y, 1 - core))

    for d in range(1, NY):
        recv("yy", d)
    agg = yb[pl.ds(2 * c, 2)]
    for d in range(1, NY):
        agg = agg + yy_r[d - 1]
    agg_ref[...] = agg.reshape(2 * BLK, BLK)

    own_b = own_b + take("rb", 3)
    for f in range(1, NX):
        own_a = own_a + take("xa", f - 1)
    gord_ref[0:BLK] = own_a
    gord_ref[BLK : 2 * BLK] = own_b
    recv("g5", 0)
    grads_ref[...] = p3_r[...]

    assert not pending, pending.keys()
    for d in started:
        d.wait_send()


def final_kernel(agg, gord, grads, nid, weight, bias, out_ref, fg_ref, wg_ref, bg_ref):
    high, low = split(agg[...])
    out_ref[...] = dot(high, weight[...]) + dot(low, weight[...]) + bias[...]
    order = jnp.where(
        lax.broadcasted_iota(jnp.int32, (2 * BLK, 2 * BLK), 0) == nid[...], 1.0, 0.0
    ).astype(BF16)
    high, low = split(gord[...])
    fg_ref[...] = dot(order, high) + dot(order, low)
    for t in range(2 * NXY):
        a, b = 8 * (t // 2), BLK * (t % 2)
        wg_ref[a : a + 8, b : b + BLK] = grads[t // NXY, t % NXY]
    tile = grads[0, NXY] + grads[1, NXY]
    bg_ref[...] = jnp.concatenate([tile[0:1], tile[1:2]], axis=1)


def body(
    features, node_ids, edge_blocks, block_rows, block_cols, block_ids, live_blocks,
    weight, bias, cotangent,
):
    vmem = pl.BlockSpec(memory_space=pltpu.VMEM)
    smem = pl.BlockSpec(memory_space=pltpu.SMEM)
    tile = (BLK, BLK)
    scratch = [
        pltpu.VMEM((8, QLEN), I32),
        pltpu.SMEM((8, QLEN), I32),
        pltpu.VMEM((64, *tile), BF16),
        pltpu.VMEM((2 * NROW + 1, *tile), BF16),
        pltpu.VMEM((2 * NCOL + 1, BLK, 2 * BLK), BF16),
        pltpu.VMEM((64, *tile), BF16),
        pltpu.VMEM((2 * BLK, BLK), BF16),
        pltpu.VMEM((BPAIRS + 1, BLK, 2 * BLK), F32),
        pltpu.VMEM((FPAIRS + 1, *tile), F32),
        pltpu.VMEM((2 * NROW, *tile), F32),
        pltpu.VMEM((2 * NCOL, *tile), F32),
        pltpu.VMEM((NCODED, MSG, BLK), I16),
        pltpu.VMEM((NCODED, MSG, BLK), I16),
        pltpu.VMEM((NY, 2, *tile), F32),
        pltpu.VMEM((NY - 1, 2, *tile), F32),
        pltpu.VMEM((2, NXY, 8, BLK), F32),
        pltpu.VMEM((NXY, 8, BLK), F32),
        pltpu.VMEM((NXY, 16, BLK), F32),
        pltpu.VMEM((NXY, 16, BLK), F32),
        pltpu.VMEM((NZ, 16, BLK), F32),
        pltpu.VMEM((2, NXY + 1, 8, BLK), F32),
        pltpu.SemaphoreType.DMA((NSEM,)),
        pltpu.SemaphoreType.DMA((NSEM,)),
        pltpu.SemaphoreType.DMA((2,)),
    ]
    agg, gord, grads = pl.pallas_call(
        main_kernel,
        out_shape=(
            jax.ShapeDtypeStruct((2 * BLK, BLK), F32),
            jax.ShapeDtypeStruct((2 * BLK, BLK), F32),
            jax.ShapeDtypeStruct((2, NXY + 1, 8, BLK), F32),
        ),
        in_specs=[smem] + [vmem] * 5 + [pl.BlockSpec(memory_space=pl.ANY)] + [vmem] * 2,
        out_specs=(vmem,) * 3,
        scratch_shapes=scratch,
        compiler_params=pltpu.CompilerParams(
            collective_id=0, has_side_effects=True, vmem_limit_bytes=58 * 2**20
        ),
    )(
        live_blocks, block_rows, block_cols, block_ids, features, node_ids, edge_blocks,
        weight, cotangent.reshape(2, BLK, 2 * BLK),
    )
    layer_out, feature_grad, weight_grad, bias_grad = pl.pallas_call(
        final_kernel,
        out_shape=(
            jax.ShapeDtypeStruct((2 * BLK, 2 * BLK), F32),
            jax.ShapeDtypeStruct((2 * BLK, BLK), F32),
            jax.ShapeDtypeStruct((BLK, 2 * BLK), F32),
            jax.ShapeDtypeStruct((1, 2 * BLK), F32),
        ),
        in_specs=[vmem] * 6,
        out_specs=(vmem,) * 4,
    )(agg, gord, grads, node_ids, weight, bias.reshape(1, -1))
    return layer_out, feature_grad, weight_grad, bias_grad.reshape(-1)


def solution(mesh):
    return jax.shard_map(
        body,
        mesh=mesh,
        in_specs=(
            P(("col", "row"), None),
            P(("col", "row"), None),
            P(),
            P("row", "col", None),
            P("row", "col", None),
            P("row", "col", None),
            P("row", "col"),
            P(),
            P(),
            P(("row", "col"), None),
        ),
        out_specs=(P(("row", "col"), None), P(("col", "row"), None), P(), P()),
        check_vma=False,
    )
```

```python
import math

import jax
import jax.numpy as jnp
from jax import lax
from jax.experimental import pallas as pl
from jax.experimental.pallas import tpu as pltpu
from jax.sharding import PartitionSpec as P

F32 = jnp.float32
BF16 = jnp.bfloat16
I16 = jnp.int16
I32 = jnp.int32
MESH = pl.DeviceIdType.MESH

NX, NZ, NY, NCORE = 4, 8, 4, 2
NROW, NCOL = NX * NZ, NY * NCORE
NXY = NX * NY
BLK = 128
SLOTS = 256
FPAIRS = (SLOTS + 2 * NCOL) // 2
BPAIRS = (SLOTS + 2 * NROW) // 2
QLEN = 384
MSG = BLK + 16
SCALE = 1.0 / 256.0


def iota(shape, dim):
    return lax.broadcasted_iota(I32, shape, dim)


def to_column(row, size):
    eye = iota((size, size), 0) == iota((size, size), 1)
    return jnp.sum(jnp.where(eye, row, 0), axis=1, keepdims=True, dtype=I32)


def sort_direction(key, code, live, zero_source, empty_pair):
    key = jnp.where(iota((1, SLOTS), 1) < live, key, 1000)
    key_col = to_column(key, SLOTS)
    code_col = to_column(code, SLOTS)
    earlier = iota((SLOTS, SLOTS), 1) < iota((SLOTS, SLOTS), 0)
    same = jnp.where((key_col == key) & earlier, 1, 0)
    rank = jnp.sum(same, axis=1, keepdims=True, dtype=I32)
    names = iota((SLOTS, 128), 1)
    count = jnp.sum(jnp.where(key_col == names, 1, 0), axis=0, keepdims=True, dtype=I32)
    padded = (count + 1) & -2
    before = jnp.sum(jnp.where(names < key_col, padded, 0), axis=1, keepdims=True, dtype=I32)
    place = jnp.where(key_col < 999, before + rank, -1)
    spot = iota((SLOTS, QLEN), 1)
    picked = jnp.sum(jnp.where(place == spot, code_col, 0), axis=0, keepdims=True, dtype=I32)
    empty = picked == 0
    ids = jnp.where(empty, 0, lax.shift_right_logical(picked - 1, 7))
    src = jnp.where(empty, zero_source, (picked - 1) & 127)
    padded_col = to_column(padded, 128)
    count_col = to_column(count, 128)
    upper = iota((128, 128), 0) < iota((128, 128), 1)
    offset = jnp.sum(jnp.where(upper, padded_col, 0), axis=0, keepdims=True, dtype=I32)
    ends = jnp.where(count > 0, lax.shift_right_logical(offset + padded, 1) - 1, empty_pair)
    offset_col = to_column(offset, 128)
    start_col = jnp.where(count_col > 0, lax.shift_right_logical(offset_col, 1), -1)
    starts = jnp.where(start_col == iota((128, QLEN), 1), 1, 0)
    keep = 1 - jnp.sum(starts, axis=0, keepdims=True, dtype=I32)
    return ids, src, keep, ends


def plan_slots(rows_ref, cols_ref, ids_ref, live_ref, out_ref):
    live = live_ref[...]
    rows = rows_ref[...].reshape(1, SLOTS)
    cols = cols_ref[...].reshape(1, SLOTS)
    ids = ids_ref[...].reshape(1, SLOTS)
    dev = lax.shift_right_logical(cols, 1)
    dev_x = lax.shift_right_logical(dev, 3)
    dev_z = dev & 7
    at_a = dev_z * NX + dev_x
    place = jnp.where((cols & 1) == 0, at_a, dev + NROW)
    f = sort_direction(rows, ids * 128 + place + 1, live, 2 * NROW, FPAIRS)
    b = sort_direction(place, ids * 128 + rows + 1, live, 2 * NCOL, BPAIRS)
    out_ref[...] = jnp.zeros((8, QLEN), I32)
    for k in range(3):
        out_ref[k : k + 1, :] = f[k]
        out_ref[3 + k : 4 + k, :] = b[k]
    out_ref[6:7, 0:128] = f[3]
    out_ref[7:8, 0:128] = b[3]


class Counter:
    def __init__(self):
        self.n = 0

    def take(self, *dims):
        base = self.n
        self.n += math.prod(dims)

        def at(*index):
            k = 0
            for d, i in zip(dims, index):
                assert 0 <= i < d
                k = k * d + i
            return base + k

        return at


def message_numbers():
    c = Counter()
    coded = dict(ra=(4, 4), la=(3, 4), xa=(3,), rb=(4,), lb=(3,), xb=(3, 8))
    plain = dict(
        ax=(4,), ar=(5, 4), al=(4, 4), br=(5,), bl=(4,), bx=(8, 4), cy=(4, 2), cs=(4, 2),
        ys=(4,), yy=(4,), g1=(1,), g2=(8,), g3=(16,), g4=(8,), g5=(1,),
    )
    table = {k: c.take(*d) for k, d in coded.items()}
    n_coded = c.n
    table.update({k: c.take(*d) for k, d in plain.items()})
    return table, n_coded, c.n


SEM, NCODED, NSEM = message_numbers()


def split(value):
    high = value.astype(BF16)
    low = (value - high.astype(F32)).astype(BF16)
    return high, low


def dot(a, b):
    return jnp.dot(a, b, preferred_element_type=F32)


def encode(value, ref):
    top = jnp.maximum(jnp.max(jnp.abs(value), axis=0, keepdims=True), 1e-30)
    e = jnp.ceil(jnp.log(top) * 256.0)
    q = jnp.round(value * (jnp.exp(e * (-1.0 / 256.0)) * 32000.0)).astype(I32)
    ref[0:BLK] = q.astype(I16)
    ref[BLK:MSG] = jnp.broadcast_to(e, (16, BLK)).astype(I32).astype(I16)


def decode(ref):
    e = ref[BLK:MSG].astype(I32).astype(F32)[0:1]
    return ref[0:BLK].astype(I32).astype(F32) * (jnp.exp(e * (1.0 / 256.0)) * (1.0 / 32000.0))


def main_kernel(
    live_h, rows_h, cols_h, ids_h, feat_h, nid_h, edge_h, weight_h, cot_h,
    agg_ref, gord_ref, grads_ref,
    live, rows, cols, ids, feat, nid, edge, weight,
    plan_v, idx, xs, cs, phl, et, sb, sf, ts, yb, sbuf, rbuf, ys_r, yy_r,
    wp, ws_r, p1_s, p1_r, p2_r, p3_r, ss, rs, ls,
):
    r = lax.axis_index("row")
    c = lax.axis_index("col")
    x, z = r // NZ, lax.rem(r, NZ)
    y, core = c // NCORE, lax.rem(c, NCORE)

    def xm(d):
        return lax.rem(x + d + NX, NX)

    def zm(d):
        return lax.rem(z + d + NZ, NZ)

    def ym(d):
        return lax.rem(y + d + NY, NY)

    def plane(px, pz):
        return (px * NZ + pz, c)

    def column(py, pc):
        return (r, py * NCORE + pc)

    def xy_peer(dx, dy):
        return (xm(dx) * NZ + z, ym(dy) * NCORE + core)

    started = []
    pending = {}

    def send(key, src, dst, dev):
        k = SEM[key[0]](*key[1:])
        d = pltpu.make_async_remote_copy(
            src_ref=src, dst_ref=dst, send_sem=ss.at[k], recv_sem=rs.at[k],
            device_id=dev, device_id_type=MESH,
        )
        d.start()
        pending[key] = d
        started.append(d)

    def recv(*key):
        pending.pop(key).wait_recv()

    xy_steps = [(a, b) for a in range(NX) for b in range(NY) if a or b]

    barrier = pltpu.get_barrier_semaphore()
    peers = [plane(x, zm(1)), plane(x, zm(-1))]
    peers += [plane(xm(d), z) for d in range(1, NX)]
    peers += [column(ym(d), core) for d in range(1, NY)]
    peers += [column(y, 1 - core)]
    for p in peers:
        pl.semaphore_signal(barrier, inc=1, device_id=p, device_id_type=MESH)
    loads = {}
    for k, (name, src, dst) in enumerate([
        ("feat", feat_h, feat), ("nid", nid_h, nid),
        ("cot", cot_h, cs.at[pl.ds(2 * c, 2)]), ("rows", rows_h, rows), ("cols", cols_h, cols),
        ("ids", ids_h, ids), ("live", live_h, live), ("weight", weight_h, weight),
        ("edge", edge_h, edge),
    ]):
        loads[name] = pltpu.make_async_copy(src, dst, ls.at[k])
        loads[name].start()

    loads["feat"].wait()
    loads["nid"].wait()
    order = jnp.where(iota((2 * BLK, 2 * BLK), 0) == nid[...], 1.0, 0.0)
    ordered = dot(feat[...].T, order.astype(BF16)).astype(BF16)
    xs[pl.ds(z * NX + x, 1)] = ordered[None, :, :BLK]
    xs[pl.ds(NROW + r, 1)] = ordered[None, :, BLK:]
    for name in ("rows", "cols", "ids", "live"):
        loads[name].wait()
    plan_slots(rows, cols, ids, live, plan_v)
    plan_copy = pltpu.make_async_copy(plan_v, idx, ls.at[len(loads)])
    plan_copy.start()
    loads["cot"].wait()
    pl.semaphore_wait(barrier, len(peers))

    def a_at(pz, px):
        return xs.at[pz * NX + px]

    def b_at(px, pz):
        return xs.at[NROW + px * NZ + pz]

    def ag_ar(s, f):
        o = a_at(zm(1 - s), xm(-f))
        send(("ar", s, f), o, o, plane(x, zm(1)))

    def ag_al(s, f):
        o = a_at(zm(s - 1), xm(-f))
        send(("al", s, f), o, o, plane(x, zm(-1)))

    def ag_br(s):
        o = b_at(x, zm(1 - s))
        send(("br", s), o, o, plane(x, zm(1)))

    def ag_bl(s):
        o = b_at(x, zm(s - 1))
        send(("bl", s), o, o, plane(x, zm(-1)))

    def ag_bx(rel):
        o = b_at(x, zm(-rel))
        for d in (2, 1, 3):
            send(("bx", rel, d), o, o, plane(xm(d), z))

    own = a_at(z, x)
    ag_br(1)
    ag_bl(1)
    for d in (2, 1, 3):
        send(("ax", d), own, own, plane(xm(d), z))
    ag_ar(1, 0)
    ag_al(1, 0)
    for h in range(2):
        o = cs.at[2 * c + h]
        for d in (2, 1, 3):
            send(("cy", d, h), o, o, column(ym(d), core))
    for h in range(2):
        o = cs.at[2 * c + h]
        send(("cs", 0, h), o, o, column(y, 1 - core))
    ag_bx(0)

    xs[2 * NROW] = jnp.zeros((BLK, BLK), BF16)
    phl[2 * NCOL] = jnp.zeros((BLK, 2 * BLK), BF16)
    sb[BPAIRS] = jnp.zeros((BLK, BLK), F32)
    sf[FPAIRS] = jnp.zeros((BLK, BLK), F32)

    def ag_b(s):
        recv("br", s)
        if s < 4:
            ag_br(s + 1)
            recv("bl", s)
            if s < 3:
                ag_bl(s + 1)
        ag_bx(s)
        if s < 4:
            ag_bx(NZ - s)

    def ag_a(s, flows=(0, 1, 3, 2)):
        for f in flows:
            recv("ar", s, f)
            if s < 4:
                ag_ar(s + 1, f)
                recv("al", s, f)
                if s < 3:
                    ag_al(s + 1, f)

    ag_b(1)
    for f in (1, 3, 2):
        recv("ax", f)
        ag_ar(1, f)
        ag_al(1, f)
    ag_a(1, (0,))
    ag_b(2)
    ag_a(1, (1, 3, 2))
    ag_a(2, (0,))
    loads["weight"].wait()
    loads["edge"].wait()

    def turn(k, carry):
        for u in range(8):
            et[8 * k + u] = edge[8 * k + u].T
        return carry

    lax.fori_loop(0, 8, turn, 0)

    for h in range(2):
        for d in (1, 3, 2):
            recv("cy", d, h)
            o = cs.at[2 * (ym(-d) * NCORE + core) + h]
            send(("cs", d, h), o, o, column(y, 1 - core))

    wt = weight[...].T

    def project(k):
        strip = cs[pl.ds(2 * k, 2)].reshape(2 * BLK, 2 * BLK)
        high, low = split(dot(strip, wt))
        both = jnp.concatenate([high, low], axis=1)
        phl[pl.ds(2 * k, 2)] = both.reshape(2, BLK, 2 * BLK)

    for d in range(NY):
        project(ym(d) * NCORE + core)
    ag_b(3)
    ag_a(2, (1, 3, 2))
    for h in range(2):
        for d in range(NY):
            recv("cs", d, h)
    for d in range(NY):
        project(ym(d) * NCORE + 1 - core)
    plan_copy.wait()

    def run_pairs(lo, hi, unroll, total, body):
        assert (hi - lo) % unroll == 0

        def step(k, total):
            for u in range(unroll):
                total = body(lo + k * unroll + u, total)
            return total

        return lax.fori_loop(0, (hi - lo) // unroll, step, total)

    def pair(base, forward, sums):
        def run(p, total):
            e0, e1 = idx[base, 2 * p], idx[base, 2 * p + 1]
            s0, s1 = idx[base + 1, 2 * p], idx[base + 1, 2 * p + 1]
            if forward:
                left = jnp.concatenate([xs[s0], xs[s1]], axis=1)
                right = jnp.concatenate([et[e0], et[e1]], axis=0)
            else:
                left = jnp.concatenate([et[e0], et[e1]], axis=1)
                right = jnp.concatenate([phl[s0], phl[s1]], axis=0)
            prod = dot(left, right)
            if prod.shape[1] == 2 * BLK:
                prod = prod[:, :BLK] + prod[:, BLK:]
            total = total * idx[base + 2, p].astype(F32) + prod
            sums[pl.ds(p, 1)] = total[None]
            return total

        return run

    back = pair(3, False, sb)
    forth = pair(0, True, sf)

    zero = jnp.zeros((BLK, BLK), F32)
    total = run_pairs(0, 80, 20, zero, back)
    ag_b(4)
    ag_a(3)
    run_pairs(80, 160, 20, total, back)

    def stage(k, carry):
        for u in range(8):
            ts[8 * k + u] = sb[idx[7, 8 * k + u]]
        return carry

    lax.fori_loop(0, 2 * NROW // 8, stage, 0)

    def t_a(pz, px):
        return pz * NX + px

    def t_b(px, pz):
        return NROW + px * NZ + pz

    def b_value(px, pz):
        return ts[t_b(px, pz)]

    def send_many(key, k, src, dst, dev):
        d = pltpu.make_async_remote_copy(
            src_ref=src, dst_ref=dst, send_sem=ss.at[k], recv_sem=rs.at[k],
            device_id=dev, device_id_type=MESH,
        )
        d.start()
        pending[key] = d
        started.append(d)

    b_order = (4, 5, 3, 6, 2, 7, 1, 0)
    b_groups = ((0, 2), (2, 4), (4, 6), (6, 8))

    def rs_bx(g):
        lo, hi = b_groups[g]
        for d in (2, 1, 3):
            base = SEM["xb"](d - 1, lo)
            for i in range(lo, hi):
                encode(b_value(xm(d), zm(b_order[i])), sbuf.at[base + i - lo])
            part = pl.ds(base, hi - lo)
            send_many(("xb", d, g), base, sbuf.at[part], rbuf.at[part], plane(xm(d), z))

    def rs_bx_recv(g):
        for d in range(1, NX):
            recv("xb", d, g)

    def rs_bg(rel):
        v = b_value(x, zm(rel))
        for d in range(1, NX):
            v = v + decode(rbuf.at[SEM["xb"](d - 1, b_order.index(rel))])
        return v

    def post(key, value, dev):
        k = SEM[key[0]](*key[1:])
        encode(value, sbuf.at[k])
        send(key, sbuf.at[k], rbuf.at[k], dev)

    def take(*key):
        recv(*key)
        return decode(rbuf.at[SEM[key[0]](*key[1:])])

    def rs_a(s):
        for f in range(NX):
            v = ts[t_a(zm(4 - s), xm(f))]
            if s:
                v = v + take("ra", s - 1, f)
            post(("ra", s, f), v, plane(x, zm(1)))
            if s < 3:
                v = ts[t_a(zm(s - 3), xm(f))]
                if s:
                    v = v + take("la", s - 1, f)
                post(("la", s, f), v, plane(x, zm(-1)))

    def rs_rb(s):
        v = rs_bg((4 - s) % NZ)
        if s:
            v = v + take("rb", s - 1)
        post(("rb", s), v, plane(x, zm(1)))

    def rs_lb(s):
        v = rs_bg((s - 3) % NZ)
        if s:
            v = v + take("lb", s - 1)
        post(("lb", s), v, plane(x, zm(-1)))

    def rs_b(s):
        rs_bx_recv(s)
        rs_rb(s)
        if s < 3:
            rs_lb(s)

    rs_bx(0)
    rs_a(0)
    for g in (1, 2, 3):
        rs_bx(g)

    ag_a(4)
    for rel in (0, 1, 7, 2, 6, 3, 5, 4):
        for d in range(1, NX):
            recv("bx", rel, d)

    run_pairs(0, 136, 17, zero, forth)

    def stage_y(k, carry):
        for u in range(4):
            yb[4 * k + u] = sf[idx[6, 4 * k + u]]
        return carry

    lax.fori_loop(0, 2 * NCOL // 4, stage_y, 0)
    def grad(k, acc):
        for u in range(2):
            at = 4 * k + 2 * u
            strip = cs[pl.ds(at, 2)].reshape(2 * BLK, 2 * BLK)
            high, low = split(jnp.concatenate([yb[at], yb[at + 1]], axis=1))
            acc = acc + dot(high, strip) + dot(low, strip)
        return acc

    acc = lax.fori_loop(0, NCOL // 2, grad, jnp.zeros((BLK, 2 * BLK), F32)) * SCALE
    for t in range(2 * NXY):
        a, b = 8 * (t // 2), BLK * (t % 2)
        wp[t // NXY, t % NXY] = acc[a : a + 8, b : b + BLK]
    send(("g1", 0), wp.at[1 - core], ws_r, column(y, 1 - core))

    for py in range(NY):
        at = 2 * (py * NCORE + 1 - core)
        send(("ys", py), yb.at[pl.ds(at, 2)], ys_r.at[py], column(y, 1 - core))

    strip = cs[pl.ds(2 * c, 2)].reshape(2 * BLK, 2 * BLK).astype(F32)
    own_bias = jnp.sum(strip, axis=0, keepdims=True) * SCALE
    bias_tile = jnp.concatenate(
        [own_bias[:, :BLK], own_bias[:, BLK:], jnp.zeros((6, BLK), F32)], axis=0
    )

    rs_a(1)
    recv("g1", 0)
    me = x * NY + y
    for t in range(NZ):
        p1_s[t, 0:8] = wp[core, 2 * t] + ws_r[2 * t]
        p1_s[t, 8:16] = wp[core, 2 * t + 1] + ws_r[2 * t + 1]
        p1_s[t, 16:24] = bias_tile
    p1_r[pl.ds(z, 1)] = p1_s[pl.ds(z, 1)]
    for d in (4, 3, 5, 2, 6, 1, 7):
        send(("g2", d), p1_s.at[zm(d)], p1_r.at[z], plane(x, zm(d)))

    rs_b(0)
    for py in range(NY):
        recv("ys", py)
    for py in range(NY):
        at = 2 * (py * NCORE + core)
        yb[pl.ds(at, 2)] = yb[pl.ds(at, 2)] + ys_r[py]
    for d in (2, 1, 3):
        at = 2 * (ym(d) * NCORE + core)
        send(("yy", d), yb.at[pl.ds(at, 2)], yy_r.at[d - 1], column(ym(d), core))

    rs_a(2)
    rs_b(1)

    for d in range(1, NZ):
        recv("g2", d)
    tile = p1_r[0]
    for k in range(1, NZ):
        tile = tile + p1_r[k]
    p2_r[pl.ds(me, 1)] = tile[None]
    for i, (a, b) in enumerate(xy_steps):
        send(("g3", i), p2_r.at[me], p2_r.at[me], xy_peer(a, b))

    rs_a(3)
    rs_b(2)

    own_a = None
    for f in (2, 1, 3, 0):
        v = ts[t_a(z, xm(f))] + take("ra", 3, f) + take("la", 2, f)
        if f:
            post(("xa", f - 1), v, plane(xm(f), z))
        else:
            own_a = v
    rs_b(3)
    own_b = rs_bg(0) + take("lb", 2)

    for i in range(len(xy_steps)):
        recv("g3", i)
    tile = p2_r[0]
    for k in range(1, NXY):
        tile = tile + p2_r[k]
    p3_r[pl.ds(core, 1), pl.ds(z, 1)] = tile[None, None, 0:16]
    p3_r[pl.ds(core, 1), NZ : NZ + 1, 0:8] = tile[None, None, 16:24]
    p3_r[pl.ds(core, 1), NZ : NZ + 1, 8:16] = jnp.zeros((1, 1, 8, BLK), F32)
    for d in (4, 3, 5, 2, 6, 1, 7):
        o = p3_r.at[core, z]
        send(("g4", d), o, o, plane(x, zm(d)))

    for d in range(1, NY):
        recv("yy", d)
    agg = yb[pl.ds(2 * c, 2)]
    for d in range(1, NY):
        agg = agg + yy_r[d - 1]
    agg_ref[0:BLK] = agg[0].T
    agg_ref[BLK : 2 * BLK] = agg[1].T

    own_b = own_b + take("rb", 3)
    for f in range(1, NX):
        own_a = own_a + take("xa", f - 1)
    gord_ref[0:BLK] = own_a
    gord_ref[BLK : 2 * BLK] = own_b

    for d in range(1, NZ):
        recv("g4", d)
    o = p3_r.at[core]
    send(("g5", 0), o, o, column(y, 1 - core))
    for d in started[:-1]:
        d.wait_send()
    recv("g5", 0)
    grads_ref[...] = p3_r[...]

    assert not pending, pending.keys()
    started[-1].wait_send()


def final_kernel(agg, gord, grads, nid, weight, bias, out_ref, fg_ref, wg_ref, bg_ref):
    high, low = split(agg[...])
    out_ref[...] = dot(high, weight[...]) + dot(low, weight[...]) + bias[...]
    order = jnp.where(
        lax.broadcasted_iota(jnp.int32, (2 * BLK, 2 * BLK), 0) == nid[...], 1.0, 0.0
    ).astype(BF16)
    high, low = split(gord[...])
    fg_ref[...] = dot(order, high) + dot(order, low)
    for t in range(2 * NXY):
        a, b = 8 * (t // 2), BLK * (t % 2)
        h, k = t // NXY, t % NXY
        wg_ref[a : a + 8, b : b + BLK] = grads[h, k // 2, 8 * (k % 2) : 8 * (k % 2) + 8]
    tile = grads[0, NZ] + grads[1, NZ]
    bg_ref[...] = jnp.concatenate([tile[0:1], tile[1:2]], axis=1)


def body(
    features, node_ids, edge_blocks, block_rows, block_cols, block_ids, live_blocks,
    weight, bias, cotangent,
):
    vmem = pl.BlockSpec(memory_space=pltpu.VMEM)
    tile = (BLK, BLK)
    scratch = [
        pltpu.VMEM((1, 1), I32),
        pltpu.VMEM((1, 1, SLOTS), I32),
        pltpu.VMEM((1, 1, SLOTS), I32),
        pltpu.VMEM((1, 1, SLOTS), I32),
        pltpu.VMEM((2 * BLK, BLK), BF16),
        pltpu.VMEM((1, 2 * BLK), I32),
        pltpu.VMEM((64, *tile), BF16),
        pltpu.VMEM((BLK, 2 * BLK), BF16),
        pltpu.VMEM((8, QLEN), I32),
        pltpu.SMEM((8, QLEN), I32),
        pltpu.VMEM((2 * NROW + 1, *tile), BF16),
        pltpu.VMEM((2 * NCOL, BLK, 2 * BLK), BF16),
        pltpu.VMEM((2 * NCOL + 1, BLK, 2 * BLK), BF16),
        pltpu.VMEM((64, *tile), BF16),
        pltpu.VMEM((BPAIRS + 1, *tile), F32),
        pltpu.VMEM((FPAIRS + 1, *tile), F32),
        pltpu.VMEM((2 * NROW, *tile), F32),
        pltpu.VMEM((2 * NCOL, *tile), F32),
        pltpu.VMEM((NCODED, MSG, BLK), I16),
        pltpu.VMEM((NCODED, MSG, BLK), I16),
        pltpu.VMEM((NY, 2, *tile), F32),
        pltpu.VMEM((NY - 1, 2, *tile), F32),
        pltpu.VMEM((2, NXY, 8, BLK), F32),
        pltpu.VMEM((NXY, 8, BLK), F32),
        pltpu.VMEM((NZ, 24, BLK), F32),
        pltpu.VMEM((NZ, 24, BLK), F32),
        pltpu.VMEM((NXY, 24, BLK), F32),
        pltpu.VMEM((2, NZ + 1, 16, BLK), F32),
        pltpu.SemaphoreType.DMA((NSEM,)),
        pltpu.SemaphoreType.DMA((NSEM,)),
        pltpu.SemaphoreType.DMA((10,)),
    ]
    agg, gord, grads = pl.pallas_call(
        main_kernel,
        out_shape=(
            jax.ShapeDtypeStruct((2 * BLK, BLK), F32),
            jax.ShapeDtypeStruct((2 * BLK, BLK), F32),
            jax.ShapeDtypeStruct((2, NZ + 1, 16, BLK), F32),
        ),
        in_specs=[pl.BlockSpec(memory_space=pl.ANY)] * 9,
        out_specs=(vmem,) * 3,
        scratch_shapes=scratch,
        compiler_params=pltpu.CompilerParams(
            collective_id=0, has_side_effects=True, vmem_limit_bytes=58 * 2**20
        ),
    )(
        live_blocks, block_rows, block_cols, block_ids, features, node_ids, edge_blocks,
        weight, cotangent.reshape(2, BLK, 2 * BLK),
    )
    layer_out, feature_grad, weight_grad, bias_grad = pl.pallas_call(
        final_kernel,
        out_shape=(
            jax.ShapeDtypeStruct((2 * BLK, 2 * BLK), F32),
            jax.ShapeDtypeStruct((2 * BLK, BLK), F32),
            jax.ShapeDtypeStruct((BLK, 2 * BLK), F32),
            jax.ShapeDtypeStruct((1, 2 * BLK), F32),
        ),
        in_specs=[vmem] * 6,
        out_specs=(vmem,) * 4,
    )(agg, gord, grads, node_ids, weight, bias.reshape(1, -1))
    return layer_out, feature_grad, weight_grad, bias_grad.reshape(-1)


def solution(mesh):
    return jax.shard_map(
        body,
        mesh=mesh,
        in_specs=(
            P(("col", "row"), None),
            P(("col", "row"), None),
            P(),
            P("row", "col", None),
            P("row", "col", None),
            P("row", "col", None),
            P("row", "col"),
            P(),
            P(),
            P(("row", "col"), None),
        ),
        out_specs=(P(("row", "col"), None), P(("col", "row"), None), P(), P()),
        check_vma=False,
    )
```

```python
import math

import jax
import jax.numpy as jnp
from jax import lax
from jax.experimental import pallas as pl
from jax.experimental.pallas import tpu as pltpu
from jax.sharding import PartitionSpec as P

F32 = jnp.float32
BF16 = jnp.bfloat16
I16 = jnp.int16
I32 = jnp.int32
MESH = pl.DeviceIdType.MESH

NX, NZ, NY, NCORE = 4, 8, 4, 2
NROW, NCOL = NX * NZ, NY * NCORE
NXY = NX * NY
BLK = 128
SLOTS = 256
FPAIRS = (SLOTS + 2 * NCOL) // 2
BPAIRS = (SLOTS + 2 * NROW) // 2
QLEN = 384
MSG = BLK + 16
SCALE = 1.0 / 256.0


def iota(shape, dim):
    return lax.broadcasted_iota(I32, shape, dim)


def to_column(row, size):
    eye = iota((size, size), 0) == iota((size, size), 1)
    return jnp.sum(jnp.where(eye, row, 0), axis=1, keepdims=True, dtype=I32)


def sort_direction(key, code, live, zero_source, empty_pair):
    key = jnp.where(iota((1, SLOTS), 1) < live, key, 1000)
    key_col = to_column(key, SLOTS)
    code_col = to_column(code, SLOTS)
    earlier = iota((SLOTS, SLOTS), 1) < iota((SLOTS, SLOTS), 0)
    same = jnp.where((key_col == key) & earlier, 1, 0)
    rank = jnp.sum(same, axis=1, keepdims=True, dtype=I32)
    names = iota((SLOTS, 128), 1)
    count = jnp.sum(jnp.where(key_col == names, 1, 0), axis=0, keepdims=True, dtype=I32)
    padded = (count + 1) & -2
    before = jnp.sum(jnp.where(names < key_col, padded, 0), axis=1, keepdims=True, dtype=I32)
    place = jnp.where(key_col < 999, before + rank, -1)
    spot = iota((SLOTS, QLEN), 1)
    picked = jnp.sum(jnp.where(place == spot, code_col, 0), axis=0, keepdims=True, dtype=I32)
    empty = picked == 0
    ids = jnp.where(empty, 0, lax.shift_right_logical(picked - 1, 7))
    src = jnp.where(empty, zero_source, (picked - 1) & 127)
    padded_col = to_column(padded, 128)
    count_col = to_column(count, 128)
    upper = iota((128, 128), 0) < iota((128, 128), 1)
    offset = jnp.sum(jnp.where(upper, padded_col, 0), axis=0, keepdims=True, dtype=I32)
    ends = jnp.where(count > 0, lax.shift_right_logical(offset + padded, 1) - 1, empty_pair)
    offset_col = to_column(offset, 128)
    start_col = jnp.where(count_col > 0, lax.shift_right_logical(offset_col, 1), -1)
    starts = jnp.where(start_col == iota((128, QLEN), 1), 1, 0)
    keep = 1 - jnp.sum(starts, axis=0, keepdims=True, dtype=I32)
    return ids, src, keep, ends


def plan_slots(rows_ref, cols_ref, ids_ref, live_ref, out_ref):
    live = live_ref[...]
    rows = rows_ref[...].reshape(1, SLOTS)
    cols = cols_ref[...].reshape(1, SLOTS)
    ids = ids_ref[...].reshape(1, SLOTS)
    dev = lax.shift_right_logical(cols, 1)
    dev_x = lax.shift_right_logical(dev, 3)
    dev_z = dev & 7
    at_a = dev_z * NX + dev_x
    place = jnp.where((cols & 1) == 0, at_a, dev + NROW)
    f = sort_direction(rows, ids * 128 + place + 1, live, 2 * NROW, FPAIRS)
    b = sort_direction(place, ids * 128 + rows + 1, live, 2 * NCOL, BPAIRS)
    out_ref[...] = jnp.zeros((8, QLEN), I32)
    for k in range(3):
        out_ref[k : k + 1, :] = f[k]
        out_ref[3 + k : 4 + k, :] = b[k]
    out_ref[6:7, 0:128] = f[3]
    out_ref[7:8, 0:128] = b[3]


class Counter:
    def __init__(self):
        self.n = 0

    def take(self, *dims):
        base = self.n
        self.n += math.prod(dims)

        def at(*index):
            k = 0
            for d, i in zip(dims, index):
                assert 0 <= i < d
                k = k * d + i
            return base + k

        return at


def message_numbers():
    c = Counter()
    coded = dict(ra=(4, 4), la=(3, 4), xa=(3,), rb=(4,), lb=(3,), xb=(3, 8))
    plain = dict(
        ax=(4,), ar=(5, 4), al=(4, 4), br=(5,), bl=(4,), bx=(8, 4), cy=(4, 2), cs=(4, 2),
        ys=(4,), yy=(4,), g1=(1,), g2=(8,), g3=(16,), g4=(8,), g5=(1,),
    )
    table = {k: c.take(*d) for k, d in coded.items()}
    n_coded = c.n
    table.update({k: c.take(*d) for k, d in plain.items()})
    return table, n_coded, c.n


SEM, NCODED, NSEM = message_numbers()


def split(value):
    high = value.astype(BF16)
    low = (value - high.astype(F32)).astype(BF16)
    return high, low


def dot(a, b):
    return jnp.dot(a, b, preferred_element_type=F32)


def encode(value, ref):
    top = jnp.maximum(jnp.max(jnp.abs(value), axis=0, keepdims=True), 1e-30)
    e = jnp.ceil(jnp.log(top) * 256.0)
    q = jnp.round(value * (jnp.exp(e * (-1.0 / 256.0)) * 32000.0)).astype(I32)
    ref[0:BLK] = q.astype(I16)
    ref[BLK:MSG] = jnp.broadcast_to(e, (16, BLK)).astype(I32).astype(I16)


def decode(ref):
    e = ref[BLK:MSG].astype(I32).astype(F32)[0:1]
    return ref[0:BLK].astype(I32).astype(F32) * (jnp.exp(e * (1.0 / 256.0)) * (1.0 / 32000.0))


def main_kernel(
    live_h, rows_h, cols_h, ids_h, feat_h, nid_h, edge_h, weight_h, cot_h, bias_h,
    out_h, fg_h, wg_h, bg_h,
    live, rows, cols, ids, feat, nid, edge, weight, bias, out_v, fg_v, wg_v, bg_v,
    plan_v, idx, xs, cs, phl, et, sb, sf, ts, yb, sbuf, rbuf, ys_r, yy_r,
    wp, ws_r, p1_s, p1_r, p2_r, p3_r, ss, rs, ls,
):
    r = lax.axis_index("row")
    c = lax.axis_index("col")
    x, z = r // NZ, lax.rem(r, NZ)
    y, core = c // NCORE, lax.rem(c, NCORE)

    def xm(d):
        return lax.rem(x + d + NX, NX)

    def zm(d):
        return lax.rem(z + d + NZ, NZ)

    def ym(d):
        return lax.rem(y + d + NY, NY)

    def plane(px, pz):
        return (px * NZ + pz, c)

    def column(py, pc):
        return (r, py * NCORE + pc)

    def xy_peer(dx, dy):
        return (xm(dx) * NZ + z, ym(dy) * NCORE + core)

    started = []
    pending = {}

    def send(key, src, dst, dev):
        k = SEM[key[0]](*key[1:])
        d = pltpu.make_async_remote_copy(
            src_ref=src, dst_ref=dst, send_sem=ss.at[k], recv_sem=rs.at[k],
            device_id=dev, device_id_type=MESH,
        )
        d.start()
        pending[key] = d
        started.append(d)

    def recv(*key):
        pending.pop(key).wait_recv()

    stores = []

    def store(src, dst):
        d = pltpu.make_async_copy(src, dst, ls.at[len(loads) + 1 + len(stores)])
        d.start()
        stores.append(d)

    xy_steps = [(a, b) for a in range(NX) for b in range(NY) if a or b]

    barrier = pltpu.get_barrier_semaphore()
    peers = [plane(x, zm(d)) for d in (2, -2, 1, -1)]
    peers += [plane(xm(d), z) for d in range(1, NX)]
    peers += [column(ym(d), core) for d in range(1, NY)]
    peers += [column(y, 1 - core)]
    for p in peers:
        pl.semaphore_signal(barrier, inc=1, device_id=p, device_id_type=MESH)
    loads = {}
    for k, (name, src, dst) in enumerate([
        ("feat", feat_h, feat), ("nid", nid_h, nid),
        ("cot", cot_h, cs.at[pl.ds(2 * c, 2)]), ("rows", rows_h, rows), ("cols", cols_h, cols),
        ("ids", ids_h, ids), ("live", live_h, live), ("weight", weight_h, weight),
        ("edge", edge_h, edge), ("bias", bias_h, bias),
    ]):
        loads[name] = pltpu.make_async_copy(src, dst, ls.at[k])
        loads[name].start()

    loads["feat"].wait()
    loads["nid"].wait()
    order = jnp.where(iota((2 * BLK, 2 * BLK), 0) == nid[...], 1.0, 0.0)
    ordered = dot(feat[...].T, order.astype(BF16)).astype(BF16)
    xs[pl.ds(z * NX + x, 1)] = ordered[None, :, :BLK]
    xs[pl.ds(NROW + r, 1)] = ordered[None, :, BLK:]
    loads["cot"].wait()
    pl.semaphore_wait(barrier, len(peers))

    def a_at(pz, px):
        return xs.at[pz * NX + px]

    def b_at(px, pz):
        return xs.at[NROW + px * NZ + pz]

    side = (1, 1, -1, -1)

    def ag_ar(s, f):
        o = a_at(zm(side[f] * (-2 if s == 4 else 1 - s)), xm(-f))
        send(("ar", s, f), o, o, plane(x, zm(side[f] * (2 if s == 4 else 1))))

    def ag_al(s, f):
        o = a_at(zm(side[f] * (s - 1)), xm(-f))
        send(("al", s, f), o, o, plane(x, zm(-side[f])))

    def ag_br(s):
        o = b_at(x, zm(-2 if s == 4 else 1 - s))
        send(("br", s), o, o, plane(x, zm(2 if s == 4 else 1)))

    def ag_bl(s):
        o = b_at(x, zm(s - 1))
        send(("bl", s), o, o, plane(x, zm(-1)))

    def ag_bx(rel):
        o = b_at(x, zm(-rel))
        for d in (2, 1, 3):
            send(("bx", rel, d), o, o, plane(xm(d), z))

    own = a_at(z, x)
    ag_br(1)
    ag_bl(1)
    for d in (2, 1, 3):
        send(("ax", d), own, own, plane(xm(d), z))
    ag_ar(1, 0)
    ag_al(1, 0)
    for h in range(2):
        o = cs.at[2 * c + h]
        for d in (2, 1, 3):
            send(("cy", d, h), o, o, column(ym(d), core))
    for h in range(2):
        o = cs.at[2 * c + h]
        send(("cs", 0, h), o, o, column(y, 1 - core))
    ag_bx(0)

    for name in ("rows", "cols", "ids", "live"):
        loads[name].wait()
    plan_slots(rows, cols, ids, live, plan_v)
    plan_copy = pltpu.make_async_copy(plan_v, idx, ls.at[len(loads)])
    plan_copy.start()
    xs[2 * NROW] = jnp.zeros((BLK, BLK), BF16)
    phl[2 * NCOL] = jnp.zeros((BLK, 2 * BLK), BF16)
    sb[BPAIRS] = jnp.zeros((BLK, BLK), F32)
    sf[FPAIRS] = jnp.zeros((BLK, BLK), F32)

    def ag_b(s):
        recv("br", s)
        if s == 2:
            ag_br(4)
        if s < 3:
            ag_br(s + 1)
        if s < 4:
            recv("bl", s)
            if s < 3:
                ag_bl(s + 1)
        ag_bx(s)
        if s < 4:
            ag_bx(NZ - s)

    def ag_a(s, flows=(0, 1, 3, 2)):
        for f in flows:
            recv("ar", s, f)
            if s == 2:
                ag_ar(4, f)
            if s < 3:
                ag_ar(s + 1, f)
            if s < 4:
                recv("al", s, f)
                if s < 3:
                    ag_al(s + 1, f)

    ag_b(1)
    for f in (1, 3, 2):
        recv("ax", f)
        ag_ar(1, f)
        ag_al(1, f)
    ag_a(1, (0,))
    ag_b(2)
    ag_a(1, (1, 3, 2))
    ag_a(2, (0,))
    loads["weight"].wait()
    loads["bias"].wait()
    loads["edge"].wait()

    def turn(k, carry):
        for u in range(8):
            et[8 * k + u] = edge[8 * k + u].T
        return carry

    lax.fori_loop(0, 8, turn, 0)

    for h in range(2):
        for d in (1, 3, 2):
            recv("cy", d, h)
            o = cs.at[2 * (ym(-d) * NCORE + core) + h]
            send(("cs", d, h), o, o, column(y, 1 - core))

    wt = weight[...].T

    def project(k):
        strip = cs[pl.ds(2 * k, 2)].reshape(2 * BLK, 2 * BLK)
        high, low = split(dot(strip, wt))
        both = jnp.concatenate([high, low], axis=1)
        phl[pl.ds(2 * k, 2)] = both.reshape(2, BLK, 2 * BLK)

    for d in range(NY):
        project(ym(d) * NCORE + core)
    ag_b(3)
    ag_a(2, (1, 3, 2))
    ag_b(4)
    for h in range(2):
        for d in range(NY):
            recv("cs", d, h)
    for d in range(NY):
        project(ym(d) * NCORE + 1 - core)
    plan_copy.wait()

    def run_pairs(lo, hi, unroll, total, body):
        assert (hi - lo) % unroll == 0

        def step(k, total):
            for u in range(unroll):
                total = body(lo + k * unroll + u, total)
            return total

        return lax.fori_loop(0, (hi - lo) // unroll, step, total)

    def pair(base, forward, sums):
        def run(p, total):
            e0, e1 = idx[base, 2 * p], idx[base, 2 * p + 1]
            s0, s1 = idx[base + 1, 2 * p], idx[base + 1, 2 * p + 1]
            if forward:
                left = jnp.concatenate([xs[s0], xs[s1]], axis=1)
                right = jnp.concatenate([et[e0], et[e1]], axis=0)
            else:
                left = jnp.concatenate([et[e0], et[e1]], axis=1)
                right = jnp.concatenate([phl[s0], phl[s1]], axis=0)
            prod = dot(left, right)
            if prod.shape[1] == 2 * BLK:
                prod = prod[:, :BLK] + prod[:, BLK:]
            total = total * idx[base + 2, p].astype(F32) + prod
            sums[pl.ds(p, 1)] = total[None]
            return total

        return run

    back = pair(3, False, sb)
    forth = pair(0, True, sf)

    zero = jnp.zeros((BLK, BLK), F32)
    run_pairs(0, 160, 40, zero, back)

    def stage(k, carry):
        for u in range(8):
            ts[8 * k + u] = sb[idx[7, 8 * k + u]]
        return carry

    lax.fori_loop(0, 2 * NROW // 8, stage, 0)

    def t_a(pz, px):
        return pz * NX + px

    def t_b(px, pz):
        return NROW + px * NZ + pz

    def b_value(px, pz):
        return ts[t_b(px, pz)]

    def send_many(key, k, src, dst, dev):
        d = pltpu.make_async_remote_copy(
            src_ref=src, dst_ref=dst, send_sem=ss.at[k], recv_sem=rs.at[k],
            device_id=dev, device_id_type=MESH,
        )
        d.start()
        pending[key] = d
        started.append(d)

    b_order = (4, 3, 5, 2, 6, 1, 7, 0)
    b_groups = ((0, 3), (3, 5), (5, 8))

    def rs_bx(g):
        lo, hi = b_groups[g]
        for d in (2, 1, 3):
            base = SEM["xb"](d - 1, lo)
            for i in range(lo, hi):
                encode(b_value(xm(d), zm(b_order[i])), sbuf.at[base + i - lo])
            part = pl.ds(base, hi - lo)
            send_many(("xb", d, g), base, sbuf.at[part], rbuf.at[part], plane(xm(d), z))

    def rs_bx_recv(g):
        for d in range(1, NX):
            recv("xb", d, g)

    def rs_bg(rel):
        v = b_value(x, zm(rel))
        for d in range(1, NX):
            v = v + decode(rbuf.at[SEM["xb"](d - 1, b_order.index(rel))])
        return v

    def post(key, value, dev):
        k = SEM[key[0]](*key[1:])
        encode(value, sbuf.at[k])
        send(key, sbuf.at[k], rbuf.at[k], dev)

    def take(*key):
        recv(*key)
        return decode(rbuf.at[SEM[key[0]](*key[1:])])

    def got(*key):
        return decode(rbuf.at[SEM[key[0]](*key[1:])])

    def rs_a(s):
        for f in (2, 0, 3, 1):
            d = side[f]
            up, up_two, down = plane(x, zm(d)), plane(x, zm(2 * d)), plane(x, zm(-d))

            def own(k):
                return ts[t_a(zm(d * k), xm(f))]

            if s == 0:
                first = [(("ra", 0, f), 4, up_two), (("ra", 1, f), 3, up), (("la", 0, f), -3, down)]
                for key, k, _ in first:
                    encode(own(k), sbuf.at[SEM[key[0]](*key[1:])])
                for key, _, dev in first:
                    k = SEM[key[0]](*key[1:])
                    send(key, sbuf.at[k], rbuf.at[k], dev)
            elif s == 1:
                recv("ra", 1, f)
                recv("ra", 0, f)
                post(("ra", 2, f), own(2) + got("ra", 0, f) + got("ra", 1, f), up)
                post(("la", 1, f), own(-2) + take("la", 0, f), down)
            else:
                post(("ra", 3, f), own(1) + take("ra", 2, f), up)
                post(("la", 2, f), own(-1) + take("la", 1, f), down)

    def rs_b(s):
        up, up_two, down = plane(x, zm(1)), plane(x, zm(2)), plane(x, zm(-1))
        rs_bx_recv(s)
        if s == 0:
            post(("rb", 0), rs_bg(4), up_two)
            post(("rb", 1), rs_bg(3), up)
            post(("lb", 0), rs_bg(5), down)
        elif s == 1:
            recv("rb", 1)
            recv("rb", 0)
            post(("rb", 2), rs_bg(2) + got("rb", 0) + got("rb", 1), up)
            post(("lb", 1), rs_bg(6) + take("lb", 0), down)
        else:
            post(("rb", 3), rs_bg(1) + take("rb", 2), up)
            post(("lb", 2), rs_bg(7) + take("lb", 1), down)

    rs_bx(0)
    rs_a(0)
    rs_bx(1)
    rs_bx(2)

    ag_a(3)
    ag_a(4)
    for rel in (0, 1, 7, 2, 6, 3, 5, 4):
        for d in range(1, NX):
            recv("bx", rel, d)

    run_pairs(0, 136, 34, zero, forth)

    acc = None
    for at in range(0, 2 * NCOL, 2):
        strip = cs[at : at + 2].reshape(2 * BLK, 2 * BLK)
        wide = jnp.concatenate([sf[idx[6, at]], sf[idx[6, at + 1]]], axis=1)
        yb[at] = wide[:, :BLK]
        yb[at + 1] = wide[:, BLK:]
        high, low = split(wide)
        part = dot(high, strip) + dot(low, strip)
        acc = part if acc is None else acc + part
    acc = acc * SCALE
    for t in range(2 * NXY):
        a, b = 8 * (t // 2), BLK * (t % 2)
        wp[t // NXY, t % NXY] = acc[a : a + 8, b : b + BLK]
    send(("g1", 0), wp.at[1 - core], ws_r, column(y, 1 - core))

    for py in range(NY):
        at = 2 * (py * NCORE + 1 - core)
        send(("ys", py), yb.at[pl.ds(at, 2)], ys_r.at[py], column(y, 1 - core))

    strip = cs[pl.ds(2 * c, 2)].reshape(2 * BLK, 2 * BLK).astype(F32)
    own_bias = jnp.sum(strip, axis=0, keepdims=True) * SCALE
    bias_tile = jnp.concatenate(
        [own_bias[:, :BLK], own_bias[:, BLK:], jnp.zeros((6, BLK), F32)], axis=0
    )

    recv("g1", 0)
    me = x * NY + y
    for t in range(NZ):
        p1_s[t, 0:8] = wp[core, 2 * t] + ws_r[2 * t]
        p1_s[t, 8:16] = wp[core, 2 * t + 1] + ws_r[2 * t + 1]
        p1_s[t, 16:24] = bias_tile
    p1_r[pl.ds(z, 1)] = p1_s[pl.ds(z, 1)]
    for d in (4, 3, 5, 2, 6, 1, 7):
        send(("g2", d), p1_s.at[zm(d)], p1_r.at[z], plane(x, zm(d)))

    rs_b(0)
    rs_a(1)
    for py in range(NY):
        recv("ys", py)
    for py in range(NY):
        at = 2 * (py * NCORE + core)
        yb[pl.ds(at, 2)] = yb[pl.ds(at, 2)] + ys_r[py]
    for d in (2, 1, 3):
        at = 2 * (ym(d) * NCORE + core)
        send(("yy", d), yb.at[pl.ds(at, 2)], yy_r.at[d - 1], column(ym(d), core))

    for d in range(1, NZ):
        recv("g2", d)
    tile = p1_r[0]
    for k in range(1, NZ):
        tile = tile + p1_r[k]
    p2_r[pl.ds(me, 1)] = tile[None]
    for i, (a, b) in enumerate(xy_steps):
        send(("g3", i), p2_r.at[me], p2_r.at[me], xy_peer(a, b))

    rs_b(1)
    rs_a(2)

    for i in range(len(xy_steps)):
        recv("g3", i)
    tile = p2_r[0]
    for k in range(1, NXY):
        tile = tile + p2_r[k]
    p3_r[pl.ds(core, 1), pl.ds(z, 1)] = tile[None, None, 0:16]
    p3_r[pl.ds(core, 1), NZ : NZ + 1, 0:8] = tile[None, None, 16:24]
    p3_r[pl.ds(core, 1), NZ : NZ + 1, 8:16] = jnp.zeros((1, 1, 8, BLK), F32)
    for d in (4, 3, 5, 2, 6, 1, 7):
        o = p3_r.at[core, z]
        send(("g4", d), o, o, plane(x, zm(d)))

    while started:
        started.pop(0).wait_send()
    rs_b(2)
    own_a = None
    for f in (2, 1, 3, 0):
        v = ts[t_a(z, xm(f))] + take("ra", 3, f) + take("la", 2, f)
        if f:
            post(("xa", f - 1), v, plane(xm(f), z))
        else:
            own_a = v
    own_b = rs_bg(0)

    for d in range(1, NY):
        recv("yy", d)
    agg = yb[pl.ds(2 * c, 2)]
    for d in range(1, NY):
        agg = agg + yy_r[d - 1]
    high, low = split(jnp.concatenate([agg[0].T, agg[1].T], axis=0))
    out_v[...] = dot(high, weight[...]) + dot(low, weight[...]) + bias[...]
    store(out_v, out_h)

    own_b = own_b + take("rb", 3) + take("lb", 2)
    for f in range(1, NX):
        own_a = own_a + take("xa", f - 1)
    high, low = split(jnp.concatenate([own_a, own_b], axis=0))
    fg_v[...] = dot(order.astype(BF16), high) + dot(order.astype(BF16), low)
    store(fg_v, fg_h)

    for d in range(1, NZ):
        recv("g4", d)
    o = p3_r.at[core]
    send(("g5", 0), o, o, column(y, 1 - core))
    recv("g5", 0)
    for t in range(2 * NXY):
        a, b = 8 * (t // 2), BLK * (t % 2)
        h, k = t // NXY, t % NXY
        wg_v[a : a + 8, b : b + BLK] = p3_r[h, k // 2, 8 * (k % 2) : 8 * (k % 2) + 8]
    tile = p3_r[0, NZ] + p3_r[1, NZ]
    bg_v[...] = jnp.concatenate([tile[0:1], tile[1:2]], axis=1)
    store(wg_v, wg_h)
    store(bg_v, bg_h)

    assert not pending, pending.keys()
    for d in started:
        d.wait_send()
    for d in stores:
        d.wait()


def copy_kernel(out_s, fg_s, wg_s, bg_s, out_h, fg_h, wg_h, bg_h, out_v, fg_v, wg_v, bg_v, sems):
    hops = [(wg_s, wg_v, wg_h), (out_s, out_v, out_h), (fg_s, fg_v, fg_h), (bg_s, bg_v, bg_h)]
    loads = [pltpu.make_async_copy(a, b, sems.at[k]) for k, (a, b, _) in enumerate(hops)]
    stores = [pltpu.make_async_copy(b, c, sems.at[4 + k]) for k, (_, b, c) in enumerate(hops)]
    for d in loads:
        d.start()
    for load, store in zip(loads, stores):
        load.wait()
        store.start()
    for d in stores:
        d.wait()


def body(
    features, node_ids, edge_blocks, block_rows, block_cols, block_ids, live_blocks,
    weight, bias, cotangent,
):
    tile = (BLK, BLK)
    scratch = [
        pltpu.VMEM((1, 1), I32),
        pltpu.VMEM((1, 1, SLOTS), I32),
        pltpu.VMEM((1, 1, SLOTS), I32),
        pltpu.VMEM((1, 1, SLOTS), I32),
        pltpu.VMEM((2 * BLK, BLK), BF16),
        pltpu.VMEM((1, 2 * BLK), I32),
        pltpu.VMEM((64, *tile), BF16),
        pltpu.VMEM((BLK, 2 * BLK), BF16),
        pltpu.VMEM((1, 2 * BLK), F32),
        pltpu.VMEM((2 * BLK, 2 * BLK), F32),
        pltpu.VMEM((2 * BLK, BLK), F32),
        pltpu.VMEM((BLK, 2 * BLK), F32),
        pltpu.VMEM((1, 2 * BLK), F32),
        pltpu.VMEM((8, QLEN), I32),
        pltpu.SMEM((8, QLEN), I32),
        pltpu.VMEM((2 * NROW + 1, *tile), BF16),
        pltpu.VMEM((2 * NCOL, BLK, 2 * BLK), BF16),
        pltpu.VMEM((2 * NCOL + 1, BLK, 2 * BLK), BF16),
        pltpu.VMEM((64, *tile), BF16),
        pltpu.VMEM((BPAIRS + 1, *tile), F32),
        pltpu.VMEM((FPAIRS + 1, *tile), F32),
        pltpu.VMEM((2 * NROW, *tile), F32),
        pltpu.VMEM((2 * NCOL, *tile), F32),
        pltpu.VMEM((NCODED, MSG, BLK), I16),
        pltpu.VMEM((NCODED, MSG, BLK), I16),
        pltpu.VMEM((NY, 2, *tile), F32),
        pltpu.VMEM((NY - 1, 2, *tile), F32),
        pltpu.VMEM((2, NXY, 8, BLK), F32),
        pltpu.VMEM((NXY, 8, BLK), F32),
        pltpu.VMEM((NZ, 24, BLK), F32),
        pltpu.VMEM((NZ, 24, BLK), F32),
        pltpu.VMEM((NXY, 24, BLK), F32),
        pltpu.VMEM((2, NZ + 1, 16, BLK), F32),
        pltpu.SemaphoreType.DMA((NSEM,)),
        pltpu.SemaphoreType.DMA((NSEM,)),
        pltpu.SemaphoreType.DMA((15,)),
    ]
    shapes = (
        jax.ShapeDtypeStruct((2 * BLK, 2 * BLK), F32),
        jax.ShapeDtypeStruct((2 * BLK, BLK), F32),
        jax.ShapeDtypeStruct((BLK, 2 * BLK), F32),
        jax.ShapeDtypeStruct((1, 2 * BLK), F32),
    )
    anywhere = pl.BlockSpec(memory_space=pl.ANY)
    results = pl.pallas_call(
        main_kernel,
        out_shape=shapes,
        in_specs=[anywhere] * 10,
        out_specs=(anywhere,) * 4,
        scratch_shapes=scratch,
        compiler_params=pltpu.CompilerParams(
            collective_id=0, has_side_effects=True, vmem_limit_bytes=58 * 2**20
        ),
    )(
        live_blocks, block_rows, block_cols, block_ids, features, node_ids, edge_blocks,
        weight, cotangent.reshape(2, BLK, 2 * BLK), bias.reshape(1, -1),
    )
    layer_out, feature_grad, weight_grad, bias_grad = pl.pallas_call(
        copy_kernel,
        out_shape=shapes,
        in_specs=[anywhere] * 4,
        out_specs=(anywhere,) * 4,
        scratch_shapes=[pltpu.VMEM(t.shape, F32) for t in shapes] + [pltpu.SemaphoreType.DMA((8,))],
    )(*results)
    return layer_out, feature_grad, weight_grad, bias_grad.reshape(-1)


def solution(mesh):
    return jax.shard_map(
        body,
        mesh=mesh,
        in_specs=(
            P(("col", "row"), None),
            P(("col", "row"), None),
            P(),
            P("row", "col", None),
            P("row", "col", None),
            P("row", "col", None),
            P("row", "col"),
            P(),
            P(),
            P(("row", "col"), None),
        ),
        out_specs=(P(("row", "col"), None), P(("col", "row"), None), P(), P()),
        check_vma=False,
    )
```

```python
import math

import jax
import jax.numpy as jnp
from jax import lax
from jax.experimental import pallas as pl
from jax.experimental.pallas import tpu as pltpu
from jax.sharding import PartitionSpec as P

F32 = jnp.float32
BF16 = jnp.bfloat16
I16 = jnp.int16
I32 = jnp.int32
MESH = pl.DeviceIdType.MESH

NX, NZ, NY, NCORE = 4, 8, 4, 2
NROW, NCOL = NX * NZ, NY * NCORE
NXY = NX * NY
BLK = 128
SLOTS = 256
FPAIRS = (SLOTS + 2 * NCOL) // 2
BPAIRS = (SLOTS + 2 * NROW) // 2
QLEN = 384
MSG = BLK + 16
SCALE = 1.0 / 256.0


def iota(shape, dim):
    return lax.broadcasted_iota(I32, shape, dim)


def to_column(row, size):
    eye = iota((size, size), 0) == iota((size, size), 1)
    return jnp.sum(jnp.where(eye, row, 0), axis=1, keepdims=True, dtype=I32)


def sort_direction(key, code, live, zero_source, empty_pair):
    key = jnp.where(iota((1, SLOTS), 1) < live, key, 1000)
    key_col = to_column(key, SLOTS)
    code_col = to_column(code, SLOTS)
    earlier = iota((SLOTS, SLOTS), 1) < iota((SLOTS, SLOTS), 0)
    same = jnp.where((key_col == key) & earlier, 1, 0)
    rank = jnp.sum(same, axis=1, keepdims=True, dtype=I32)
    names = iota((SLOTS, 128), 1)
    count = jnp.sum(jnp.where(key_col == names, 1, 0), axis=0, keepdims=True, dtype=I32)
    padded = (count + 1) & -2
    before = jnp.sum(jnp.where(names < key_col, padded, 0), axis=1, keepdims=True, dtype=I32)
    place = jnp.where(key_col < 999, before + rank, -1)
    spot = iota((SLOTS, QLEN), 1)
    picked = jnp.sum(jnp.where(place == spot, code_col, 0), axis=0, keepdims=True, dtype=I32)
    empty = picked == 0
    ids = jnp.where(empty, 0, lax.shift_right_logical(picked - 1, 7))
    src = jnp.where(empty, zero_source, (picked - 1) & 127)
    padded_col = to_column(padded, 128)
    count_col = to_column(count, 128)
    upper = iota((128, 128), 0) < iota((128, 128), 1)
    offset = jnp.sum(jnp.where(upper, padded_col, 0), axis=0, keepdims=True, dtype=I32)
    ends = jnp.where(count > 0, lax.shift_right_logical(offset + padded, 1) - 1, empty_pair)
    offset_col = to_column(offset, 128)
    start_col = jnp.where(count_col > 0, lax.shift_right_logical(offset_col, 1), -1)
    starts = jnp.where(start_col == iota((128, QLEN), 1), 1, 0)
    keep = 1 - jnp.sum(starts, axis=0, keepdims=True, dtype=I32)
    return ids, src, keep, ends


def plan_slots(rows_ref, cols_ref, ids_ref, live_ref, out_ref):
    live = live_ref[...]
    rows = rows_ref[...].reshape(1, SLOTS)
    cols = cols_ref[...].reshape(1, SLOTS)
    ids = ids_ref[...].reshape(1, SLOTS)
    dev = lax.shift_right_logical(cols, 1)
    dev_x = lax.shift_right_logical(dev, 3)
    dev_z = dev & 7
    at_a = dev_z * NX + dev_x
    place = jnp.where((cols & 1) == 0, at_a, dev + NROW)
    f = sort_direction(rows, ids * 128 + place + 1, live, 2 * NROW, FPAIRS)
    b = sort_direction(place, ids * 128 + rows + 1, live, 2 * NCOL, BPAIRS)
    out_ref[...] = jnp.zeros((8, QLEN), I32)
    for k in range(3):
        out_ref[k : k + 1, :] = f[k]
        out_ref[3 + k : 4 + k, :] = b[k]
    out_ref[6:7, 0:128] = f[3]
    out_ref[7:8, 0:128] = b[3]


class Counter:
    def __init__(self):
        self.n = 0

    def take(self, *dims):
        base = self.n
        self.n += math.prod(dims)

        def at(*index):
            k = 0
            for d, i in zip(dims, index):
                assert 0 <= i < d
                k = k * d + i
            return base + k

        return at


def message_numbers():
    c = Counter()
    coded = dict(ra=(4, 4), la=(3, 4), xa=(3,), rb=(4,), lb=(3,), xb=(3, 8))
    plain = dict(
        ax=(4,), ar=(5, 4), al=(4, 4), br=(5,), bl=(4,), bx=(8, 4), cy=(4, 2), cs=(4, 2),
        ys=(4,), yy=(4,), g1=(1,), g2=(8,), g3=(16,), g4=(8,), g5=(1,),
    )
    table = {k: c.take(*d) for k, d in coded.items()}
    n_coded = c.n
    table.update({k: c.take(*d) for k, d in plain.items()})
    return table, n_coded, c.n


SEM, NCODED, NSEM = message_numbers()


def split(value):
    high = value.astype(BF16)
    low = (value - high.astype(F32)).astype(BF16)
    return high, low


def dot(a, b):
    return jnp.dot(a, b, preferred_element_type=F32)


def encode(value, ref):
    top = jnp.maximum(jnp.max(jnp.abs(value), axis=0, keepdims=True), 1e-30)
    e = jnp.ceil(jnp.log(top) * 256.0)
    q = jnp.round(value * (jnp.exp(e * (-1.0 / 256.0)) * 32000.0)).astype(I32)
    ref[0:BLK] = q.astype(I16)
    ref[BLK:MSG] = jnp.broadcast_to(e, (16, BLK)).astype(I32).astype(I16)


def decode(ref):
    e = ref[BLK:MSG].astype(I32).astype(F32)[0:1]
    return ref[0:BLK].astype(I32).astype(F32) * (jnp.exp(e * (1.0 / 256.0)) * (1.0 / 32000.0))


def main_kernel(
    live_h, rows_h, cols_h, ids_h, feat_h, nid_h, edge_h, weight_h, cot_h, bias_h,
    out_h, fg_h, wg_h, bg_h,
    live, rows, cols, ids, feat, nid, edge, weight, bias, out_v, fg_v, wg_v, bg_v,
    plan_v, idx, xs, cs, phl, et, sb, sf, yb, sbuf, rbuf, ys_r, yy_r,
    wp, ws_r, p1_s, p1_r, p2_r, p3_r, ss, rs, ls,
):
    r = lax.axis_index("row")
    c = lax.axis_index("col")
    x, z = r // NZ, lax.rem(r, NZ)
    y, core = c // NCORE, lax.rem(c, NCORE)

    def xm(d):
        return lax.rem(x + d + NX, NX)

    def zm(d):
        return lax.rem(z + d + NZ, NZ)

    def ym(d):
        return lax.rem(y + d + NY, NY)

    def plane(px, pz):
        return (px * NZ + pz, c)

    def column(py, pc):
        return (r, py * NCORE + pc)

    def xy_peer(dx, dy):
        return (xm(dx) * NZ + z, ym(dy) * NCORE + core)

    started = []
    pending = {}

    def send(key, src, dst, dev):
        k = SEM[key[0]](*key[1:])
        d = pltpu.make_async_remote_copy(
            src_ref=src, dst_ref=dst, send_sem=ss.at[k], recv_sem=rs.at[k],
            device_id=dev, device_id_type=MESH,
        )
        d.start()
        pending[key] = d
        started.append(d)

    def recv(*key):
        pending.pop(key).wait_recv()

    stores = []

    def store(src, dst):
        d = pltpu.make_async_copy(src, dst, ls.at[len(loads) + 1 + len(stores)])
        d.start()
        stores.append(d)

    xy_steps = [(a, b) for a in range(NX) for b in range(NY) if a or b]

    barrier = pltpu.get_barrier_semaphore()
    peers = [plane(x, zm(d)) for d in (2, -2, 1, -1)]
    peers += [plane(xm(d), z) for d in range(1, NX)]
    peers += [column(ym(d), core) for d in range(1, NY)]
    peers += [column(y, 1 - core)]
    for p in peers:
        pl.semaphore_signal(barrier, inc=1, device_id=p, device_id_type=MESH)
    loads = {}
    for k, (name, src, dst) in enumerate([
        ("feat", feat_h, feat), ("nid", nid_h, nid),
        ("cot", cot_h, cs.at[pl.ds(2 * c, 2)]), ("rows", rows_h, rows), ("cols", cols_h, cols),
        ("ids", ids_h, ids), ("live", live_h, live), ("weight", weight_h, weight),
        ("edge", edge_h, edge), ("bias", bias_h, bias),
    ]):
        loads[name] = pltpu.make_async_copy(src, dst, ls.at[k])
        loads[name].start()

    loads["feat"].wait()
    loads["nid"].wait()
    order = jnp.where(iota((2 * BLK, 2 * BLK), 0) == nid[...], 1.0, 0.0)
    ordered = dot(feat[...].T, order.astype(BF16)).astype(BF16)
    xs[pl.ds(z * NX + x, 1)] = ordered[None, :, :BLK]
    xs[pl.ds(NROW + r, 1)] = ordered[None, :, BLK:]
    loads["cot"].wait()
    pl.semaphore_wait(barrier, len(peers))

    def a_at(pz, px):
        return xs.at[pz * NX + px]

    def b_at(px, pz):
        return xs.at[NROW + px * NZ + pz]

    side = (1, 1, -1, -1)

    def ag_ar(s, f):
        o = a_at(zm(side[f] * (-2 if s == 4 else 1 - s)), xm(-f))
        send(("ar", s, f), o, o, plane(x, zm(side[f] * (2 if s == 4 else 1))))

    def ag_al(s, f):
        o = a_at(zm(side[f] * (s - 1)), xm(-f))
        send(("al", s, f), o, o, plane(x, zm(-side[f])))

    def ag_br(s):
        o = b_at(x, zm(-2 if s == 4 else 1 - s))
        send(("br", s), o, o, plane(x, zm(2 if s == 4 else 1)))

    def ag_bl(s):
        o = b_at(x, zm(s - 1))
        send(("bl", s), o, o, plane(x, zm(-1)))

    def ag_bx(rel):
        o = b_at(x, zm(-rel))
        for d in (2, 1, 3):
            send(("bx", rel, d), o, o, plane(xm(d), z))

    for h in range(2):
        o = cs.at[2 * c + h]
        for d in (2, 1, 3):
            send(("cy", d, h), o, o, column(ym(d), core))
    own = a_at(z, x)
    ag_br(1)
    ag_bl(1)
    for d in (2, 1, 3):
        send(("ax", d), own, own, plane(xm(d), z))
    ag_ar(1, 0)
    ag_al(1, 0)
    for h in range(2):
        o = cs.at[2 * c + h]
        send(("cs", 0, h), o, o, column(y, 1 - core))
    ag_bx(0)

    for name in ("rows", "cols", "ids", "live"):
        loads[name].wait()
    plan_slots(rows, cols, ids, live, plan_v)
    plan_copy = pltpu.make_async_copy(plan_v, idx, ls.at[len(loads)])
    plan_copy.start()
    xs[2 * NROW] = jnp.zeros((BLK, BLK), BF16)
    phl[2 * NCOL] = jnp.zeros((BLK, 2 * BLK), BF16)
    sb[BPAIRS] = jnp.zeros((BLK, BLK), F32)
    sf[FPAIRS] = jnp.zeros((BLK, BLK), F32)

    def ag_b(s):
        recv("br", s)
        if s == 2:
            ag_br(4)
        if s < 3:
            ag_br(s + 1)
        if s < 4:
            recv("bl", s)
            if s < 3:
                ag_bl(s + 1)
        ag_bx(s)
        if s < 4:
            ag_bx(NZ - s)

    def ag_a(s, flows=(0, 1, 3, 2)):
        for f in flows:
            recv("ar", s, f)
            if s == 2:
                ag_ar(4, f)
            if s < 3:
                ag_ar(s + 1, f)
            if s < 4:
                recv("al", s, f)
                if s < 3:
                    ag_al(s + 1, f)

    ag_b(1)
    for f in (1, 3, 2):
        recv("ax", f)
        ag_ar(1, f)
        ag_al(1, f)
    ag_a(1, (0,))
    ag_b(2)
    ag_a(1, (1, 3, 2))
    ag_a(2, (0,))
    loads["weight"].wait()
    loads["bias"].wait()
    loads["edge"].wait()

    def turn(k, carry):
        for u in range(8):
            et[8 * k + u] = edge[8 * k + u].T
        return carry

    lax.fori_loop(0, 8, turn, 0)

    for h in range(2):
        for d in (1, 3, 2):
            recv("cy", d, h)
            o = cs.at[2 * (ym(-d) * NCORE + core) + h]
            send(("cs", d, h), o, o, column(y, 1 - core))

    wt = weight[...].T

    def project(k):
        strip = cs[pl.ds(2 * k, 2)].reshape(2 * BLK, 2 * BLK)
        high, low = split(dot(strip, wt))
        both = jnp.concatenate([high, low], axis=1)
        phl[pl.ds(2 * k, 2)] = both.reshape(2, BLK, 2 * BLK)

    for d in range(NY):
        project(ym(d) * NCORE + core)
    ag_b(3)
    ag_a(2, (1, 3, 2))
    ag_b(4)
    for h in range(2):
        for d in range(NY):
            recv("cs", d, h)
    for d in range(NY):
        project(ym(d) * NCORE + 1 - core)
    plan_copy.wait()

    def run_pairs(lo, hi, unroll, total, body):
        assert (hi - lo) % unroll == 0

        def step(k, total):
            for u in range(unroll):
                total = body(lo + k * unroll + u, total)
            return total

        return lax.fori_loop(0, (hi - lo) // unroll, step, total)

    def pair(base, forward, sums):
        def run(p, total):
            e0, e1 = idx[base, 2 * p], idx[base, 2 * p + 1]
            s0, s1 = idx[base + 1, 2 * p], idx[base + 1, 2 * p + 1]
            if forward:
                left = jnp.concatenate([xs[s0], xs[s1]], axis=1)
                right = jnp.concatenate([et[e0], et[e1]], axis=0)
            else:
                left = jnp.concatenate([et[e0], et[e1]], axis=1)
                right = jnp.concatenate([phl[s0], phl[s1]], axis=0)
            prod = dot(left, right)
            if prod.shape[1] == 2 * BLK:
                prod = prod[:, :BLK] + prod[:, BLK:]
            total = total * idx[base + 2, p].astype(F32) + prod
            sums[pl.ds(p, 1)] = total[None]
            return total

        return run

    back = pair(3, False, sb)
    forth = pair(0, True, sf)

    zero = jnp.zeros((BLK, BLK), F32)
    run_pairs(0, 160, 40, zero, back)

    def product(at):
        return sb[idx[7, at]]

    def t_a(pz, px):
        return pz * NX + px

    def t_b(px, pz):
        return NROW + px * NZ + pz

    def b_value(px, pz):
        return product(t_b(px, pz))

    def send_many(key, k, src, dst, dev):
        d = pltpu.make_async_remote_copy(
            src_ref=src, dst_ref=dst, send_sem=ss.at[k], recv_sem=rs.at[k],
            device_id=dev, device_id_type=MESH,
        )
        d.start()
        pending[key] = d
        started.append(d)

    b_order = (4, 3, 5, 2, 6, 1, 7, 0)
    b_groups = ((0, 3), (3, 5), (5, 8))

    def rs_bx(g):
        lo, hi = b_groups[g]
        for d in (2, 1, 3):
            base = SEM["xb"](d - 1, lo)
            for i in range(lo, hi):
                encode(b_value(xm(d), zm(b_order[i])), sbuf.at[base + i - lo])
            part = pl.ds(base, hi - lo)
            send_many(("xb", d, g), base, sbuf.at[part], rbuf.at[part], plane(xm(d), z))

    def rs_bx_recv(g):
        for d in range(1, NX):
            recv("xb", d, g)

    def rs_bg(rel):
        v = b_value(x, zm(rel))
        for d in range(1, NX):
            v = v + decode(rbuf.at[SEM["xb"](d - 1, b_order.index(rel))])
        return v

    def post(key, value, dev):
        k = SEM[key[0]](*key[1:])
        encode(value, sbuf.at[k])
        send(key, sbuf.at[k], rbuf.at[k], dev)

    def take(*key):
        recv(*key)
        return decode(rbuf.at[SEM[key[0]](*key[1:])])

    def got(*key):
        return decode(rbuf.at[SEM[key[0]](*key[1:])])

    def rs_a(s):
        for f in (2, 0, 3, 1):
            d = side[f]
            up, up_two, down = plane(x, zm(d)), plane(x, zm(2 * d)), plane(x, zm(-d))

            def own(k):
                return product(t_a(zm(d * k), xm(f)))

            if s == 0:
                first = [(("ra", 0, f), 4, up_two), (("ra", 1, f), 3, up), (("la", 0, f), -3, down)]
                for key, k, _ in first:
                    encode(own(k), sbuf.at[SEM[key[0]](*key[1:])])
                for key, _, dev in first:
                    k = SEM[key[0]](*key[1:])
                    send(key, sbuf.at[k], rbuf.at[k], dev)
            elif s == 1:
                recv("ra", 1, f)
                recv("ra", 0, f)
                post(("ra", 2, f), own(2) + got("ra", 0, f) + got("ra", 1, f), up)
                post(("la", 1, f), own(-2) + take("la", 0, f), down)
            else:
                post(("ra", 3, f), own(1) + take("ra", 2, f), up)
                post(("la", 2, f), own(-1) + take("la", 1, f), down)

    def rs_b(s):
        up, up_two, down = plane(x, zm(1)), plane(x, zm(2)), plane(x, zm(-1))
        rs_bx_recv(s)
        if s == 0:
            post(("rb", 0), rs_bg(4), up_two)
            post(("rb", 1), rs_bg(3), up)
            post(("lb", 0), rs_bg(5), down)
        elif s == 1:
            recv("rb", 1)
            recv("rb", 0)
            post(("rb", 2), rs_bg(2) + got("rb", 0) + got("rb", 1), up)
            post(("lb", 1), rs_bg(6) + take("lb", 0), down)
        else:
            post(("rb", 3), rs_bg(1) + take("rb", 2), up)
            post(("lb", 2), rs_bg(7) + take("lb", 1), down)

    rs_a(0)
    rs_bx(0)
    rs_bx(1)

    ag_a(3)
    ag_a(4)
    for rel in (0, 1, 7, 2, 6, 3, 5, 4):
        for d in range(1, NX):
            recv("bx", rel, d)

    run_pairs(0, 136, 34, zero, forth)

    acc = None
    for at in range(0, 2 * NCOL, 2):
        strip = cs[at : at + 2].reshape(2 * BLK, 2 * BLK)
        wide = jnp.concatenate([sf[idx[6, at]], sf[idx[6, at + 1]]], axis=1)
        yb[at] = wide[:, :BLK]
        yb[at + 1] = wide[:, BLK:]
        high, low = split(wide)
        part = dot(high, strip) + dot(low, strip)
        acc = part if acc is None else acc + part
    acc = acc * SCALE
    for t in range(2 * NXY):
        a, b = 8 * (t // 2), BLK * (t % 2)
        wp[t // NXY, t % NXY] = acc[a : a + 8, b : b + BLK]
    send(("g1", 0), wp.at[1 - core], ws_r, column(y, 1 - core))

    for py in range(NY):
        at = 2 * (py * NCORE + 1 - core)
        send(("ys", py), yb.at[pl.ds(at, 2)], ys_r.at[py], column(y, 1 - core))

    strip = cs[pl.ds(2 * c, 2)].reshape(2 * BLK, 2 * BLK).astype(F32)
    own_bias = jnp.sum(strip, axis=0, keepdims=True) * SCALE
    bias_tile = jnp.concatenate(
        [own_bias[:, :BLK], own_bias[:, BLK:], jnp.zeros((6, BLK), F32)], axis=0
    )

    recv("g1", 0)
    me = x * NY + y
    for t in range(NZ):
        p1_s[t, 0:8] = wp[core, 2 * t] + ws_r[2 * t]
        p1_s[t, 8:16] = wp[core, 2 * t + 1] + ws_r[2 * t + 1]
        p1_s[t, 16:24] = bias_tile
    p1_r[pl.ds(z, 1)] = p1_s[pl.ds(z, 1)]
    for d in (4, 3, 5, 2, 6, 1, 7):
        send(("g2", d), p1_s.at[zm(d)], p1_r.at[z], plane(x, zm(d)))

    rs_bx(2)
    rs_b(0)
    rs_a(1)
    for py in range(NY):
        recv("ys", py)
    for py in range(NY):
        at = 2 * (py * NCORE + core)
        yb[pl.ds(at, 2)] = yb[pl.ds(at, 2)] + ys_r[py]
    for d in (2, 1, 3):
        at = 2 * (ym(d) * NCORE + core)
        send(("yy", d), yb.at[pl.ds(at, 2)], yy_r.at[d - 1], column(ym(d), core))

    for d in range(1, NZ):
        recv("g2", d)
    tile = p1_r[0]
    for k in range(1, NZ):
        tile = tile + p1_r[k]
    p2_r[pl.ds(me, 1)] = tile[None]
    for i, (a, b) in enumerate(xy_steps):
        send(("g3", i), p2_r.at[me], p2_r.at[me], xy_peer(a, b))

    rs_b(1)
    rs_a(2)

    for i in range(len(xy_steps)):
        recv("g3", i)
    tile = p2_r[0]
    for k in range(1, NXY):
        tile = tile + p2_r[k]
    p3_r[pl.ds(core, 1), pl.ds(z, 1)] = tile[None, None, 0:16]
    p3_r[pl.ds(core, 1), NZ : NZ + 1, 0:8] = tile[None, None, 16:24]
    p3_r[pl.ds(core, 1), NZ : NZ + 1, 8:16] = jnp.zeros((1, 1, 8, BLK), F32)
    for d in (4, 3, 5, 2, 6, 1, 7):
        o = p3_r.at[core, z]
        send(("g4", d), o, o, plane(x, zm(d)))

    while started:
        started.pop(0).wait_send()
    rs_b(2)
    own_a = None
    for f in (2, 1, 3, 0):
        v = product(t_a(z, xm(f))) + take("ra", 3, f) + take("la", 2, f)
        if f:
            post(("xa", f - 1), v, plane(xm(f), z))
        else:
            own_a = v
    own_b = rs_bg(0)

    for d in range(1, NY):
        recv("yy", d)
    agg = yb[pl.ds(2 * c, 2)]
    for d in range(1, NY):
        agg = agg + yy_r[d - 1]
    high, low = split(jnp.concatenate([agg[0].T, agg[1].T], axis=0))
    out_v[...] = dot(high, weight[...]) + dot(low, weight[...]) + bias[...]
    store(out_v, out_h)

    own_b = own_b + take("rb", 3) + take("lb", 2)
    for f in range(1, NX):
        own_a = own_a + take("xa", f - 1)
    high, low = split(jnp.concatenate([own_a, own_b], axis=0))
    fg_v[...] = dot(order.astype(BF16), high) + dot(order.astype(BF16), low)
    store(fg_v, fg_h)

    for d in range(1, NZ):
        recv("g4", d)
    o = p3_r.at[core]
    send(("g5", 0), o, o, column(y, 1 - core))
    recv("g5", 0)
    for t in range(2 * NXY):
        a, b = 8 * (t // 2), BLK * (t % 2)
        h, k = t // NXY, t % NXY
        wg_v[a : a + 8, b : b + BLK] = p3_r[h, k // 2, 8 * (k % 2) : 8 * (k % 2) + 8]
    tile = p3_r[0, NZ] + p3_r[1, NZ]
    bg_v[...] = jnp.concatenate([tile[0:1], tile[1:2]], axis=1)
    store(wg_v, wg_h)
    store(bg_v, bg_h)

    assert not pending, pending.keys()
    for d in started:
        d.wait_send()
    for d in stores:
        d.wait()


def copy_kernel(out_s, fg_s, wg_s, bg_s, out_h, fg_h, wg_h, bg_h, out_v, fg_v, wg_v, bg_v, sems):
    hops = [(wg_s, wg_v, wg_h), (out_s, out_v, out_h), (fg_s, fg_v, fg_h), (bg_s, bg_v, bg_h)]
    loads = [pltpu.make_async_copy(a, b, sems.at[k]) for k, (a, b, _) in enumerate(hops)]
    stores = [pltpu.make_async_copy(b, c, sems.at[4 + k]) for k, (_, b, c) in enumerate(hops)]
    for d in loads:
        d.start()
    for load, store in zip(loads, stores):
        load.wait()
        store.start()
    for d in stores:
        d.wait()


def body(
    features, node_ids, edge_blocks, block_rows, block_cols, block_ids, live_blocks,
    weight, bias, cotangent,
):
    tile = (BLK, BLK)
    scratch = [
        pltpu.VMEM((1, 1), I32),
        pltpu.VMEM((1, 1, SLOTS), I32),
        pltpu.VMEM((1, 1, SLOTS), I32),
        pltpu.VMEM((1, 1, SLOTS), I32),
        pltpu.VMEM((2 * BLK, BLK), BF16),
        pltpu.VMEM((1, 2 * BLK), I32),
        pltpu.VMEM((64, *tile), BF16),
        pltpu.VMEM((BLK, 2 * BLK), BF16),
        pltpu.VMEM((1, 2 * BLK), F32),
        pltpu.VMEM((2 * BLK, 2 * BLK), F32),
        pltpu.VMEM((2 * BLK, BLK), F32),
        pltpu.VMEM((BLK, 2 * BLK), F32),
        pltpu.VMEM((1, 2 * BLK), F32),
        pltpu.VMEM((8, QLEN), I32),
        pltpu.SMEM((8, QLEN), I32),
        pltpu.VMEM((2 * NROW + 1, *tile), BF16),
        pltpu.VMEM((2 * NCOL, BLK, 2 * BLK), BF16),
        pltpu.VMEM((2 * NCOL + 1, BLK, 2 * BLK), BF16),
        pltpu.VMEM((64, *tile), BF16),
        pltpu.VMEM((BPAIRS + 1, *tile), F32),
        pltpu.VMEM((FPAIRS + 1, *tile), F32),
        pltpu.VMEM((2 * NCOL, *tile), F32),
        pltpu.VMEM((NCODED, MSG, BLK), I16),
        pltpu.VMEM((NCODED, MSG, BLK), I16),
        pltpu.VMEM((NY, 2, *tile), F32),
        pltpu.VMEM((NY - 1, 2, *tile), F32),
        pltpu.VMEM((2, NXY, 8, BLK), F32),
        pltpu.VMEM((NXY, 8, BLK), F32),
        pltpu.VMEM((NZ, 24, BLK), F32),
        pltpu.VMEM((NZ, 24, BLK), F32),
        pltpu.VMEM((NXY, 24, BLK), F32),
        pltpu.VMEM((2, NZ + 1, 16, BLK), F32),
        pltpu.SemaphoreType.DMA((NSEM,)),
        pltpu.SemaphoreType.DMA((NSEM,)),
        pltpu.SemaphoreType.DMA((15,)),
    ]
    shapes = (
        jax.ShapeDtypeStruct((2 * BLK, 2 * BLK), F32),
        jax.ShapeDtypeStruct((2 * BLK, BLK), F32),
        jax.ShapeDtypeStruct((BLK, 2 * BLK), F32),
        jax.ShapeDtypeStruct((1, 2 * BLK), F32),
    )
    anywhere = pl.BlockSpec(memory_space=pl.ANY)
    results = pl.pallas_call(
        main_kernel,
        out_shape=shapes,
        in_specs=[anywhere] * 10,
        out_specs=(anywhere,) * 4,
        scratch_shapes=scratch,
        compiler_params=pltpu.CompilerParams(
            collective_id=0, has_side_effects=True, vmem_limit_bytes=58 * 2**20
        ),
    )(
        live_blocks, block_rows, block_cols, block_ids, features, node_ids, edge_blocks,
        weight, cotangent.reshape(2, BLK, 2 * BLK), bias.reshape(1, -1),
    )
    layer_out, feature_grad, weight_grad, bias_grad = pl.pallas_call(
        copy_kernel,
        out_shape=shapes,
        in_specs=[anywhere] * 4,
        out_specs=(anywhere,) * 4,
        scratch_shapes=[pltpu.VMEM(t.shape, F32) for t in shapes] + [pltpu.SemaphoreType.DMA((8,))],
    )(*results)
    return layer_out, feature_grad, weight_grad, bias_grad.reshape(-1)


def solution(mesh):
    return jax.shard_map(
        body,
        mesh=mesh,
        in_specs=(
            P(("col", "row"), None),
            P(("col", "row"), None),
            P(),
            P("row", "col", None),
            P("row", "col", None),
            P("row", "col", None),
            P("row", "col"),
            P(),
            P(),
            P(("row", "col"), None),
        ),
        out_specs=(P(("row", "col"), None), P(("col", "row"), None), P(), P()),
        check_vma=False,
    )
```
